128 devices in a mesh: ctx: 128 (over x, z, y, core).
Axes of the slice: x: 4, y: 4, z: 4, core: 2. Of those that a mesh axis runs over, the one named last changes fastest.
Arguments:
- inputs: bfloat16 [16384, 4096], P('ctx'), may hold values from -24 to 24
- streams: bfloat16 [3, 4096, 16384], P(None, None, 'ctx'), may hold values from -6 to 6
- short_filter: float32 [3, 3, 4096], replicated, may hold values from -3.5 to 3.5
- long_filter: float32 [4096, 16384], P('ctx'), may hold values from -0.046875 to 0.046875
- skip_gain: float32 [4096], P('ctx'), may hold values from -4 to 4
Outputs:
- gated: bfloat16 [4096, 16384], P(None, 'ctx')
- input_gram: float32 [512, 8, 512], P('ctx')
- output_gram: float32 [512, 8, 512], P('ctx')
The draws below stay inside these ranges and needn't reach their ends.
All inputs are finite; a program needn't handle non-finite values.
Results may differ from the reference program's by a relative error of at most 0.0076.
Values may be sent and summed in bfloat16 or wider, within the bound.
A program may use at most 128 MiB of HBM per device.

```python
import jax
import jax.numpy as jnp
from jax import lax

D = 4096
BLOCK = 512
SHORT = 3
LENGTH = 16384


def with_spikes(entries, stream_key, source, target, blocks, factor):
    owner, partner = [(jnp.arange(entries.shape[axis_at]) // (entries.shape[axis_at] // blocks)).reshape([-1 if axis == axis_at else 1 for axis in range(entries.ndim)]) for axis_at in (source, target)]
    chosen = jax.random.permutation(stream_key, blocks)[partner]
    strong = (owner == chosen) | (owner == (partner + blocks // 2) % blocks)
    return jnp.where(strong, factor * entries, entries)


def block_scale(rng, extent, shards, least, high):
    gain = 1.0
    for axis_at, shards_of in shards:
        draws = jax.random.uniform(jax.random.fold_in(jax.random.fold_in(rng, 6), axis_at), (shards_of,), jnp.float32, least / len(shards), high / len(shards))
        gain = gain * jnp.repeat(jnp.exp(draws), extent[axis_at] // shards_of).reshape((-1,) + (1,) * (len(extent) - 1 - axis_at))
    return gain


def centred(rng, shape, scale, limit, cuts=(), held_as=jnp.bfloat16):
    level = block_scale(rng, shape, cuts, -0.22, 0.18) if cuts else 1.0
    values = jax.random.normal(rng, shape, jnp.float32) * scale * level
    return jnp.minimum(jnp.maximum(values, -limit), limit).astype(held_as)


def noise_with(stream_key, dims, width, limit, cuts, heavy, dtype=jnp.bfloat16):
    drawn = width * jax.random.normal(stream_key, dims, jnp.float32)
    if cuts:
        drawn = drawn * block_scale(stream_key, dims, cuts, -0.22, 0.18)
    return jnp.clip(with_spikes(drawn, jax.random.fold_in(stream_key, 3), *heavy), -limit, limit).astype(dtype)


def setup_inputs(seed: int = 0) -> dict:
    key_of = jax.random.split(jax.random.key(seed), 6)
    return {
        "inputs": noise_with(key_of[0], (LENGTH, D), 1.0, 24.0, ((0, 128),), (0, 1, 128, 5.5)),
        "streams": centred(key_of[1], (3, D, LENGTH), 1.0, 6.0, ((2, 128),)),
        "short_filter": centred(key_of[2], (3, SHORT, D), SHORT ** -0.5, 3.5, (), jnp.float32),
        "long_filter": centred(key_of[3], (D, LENGTH), LENGTH ** -0.5, 0.046875, ((0, 128),), jnp.float32),
        "skip_gain": centred(key_of[4], (D,), 1.0, 4.0, ((0, 128),), jnp.float32),
    }


def short_mix(streams, short_filter):
    seq_length = streams.shape[2]
    values = streams.astype(jnp.float32)
    padded = jnp.pad(values, ((0, 0), (0, 0), (SHORT - 1, 0)))
    total = jnp.zeros(values.shape, jnp.float32)
    for offset in range(SHORT):
        begin = SHORT - 1 - offset
        total = total + short_filter[:, offset, :, None] * padded[:, :, begin:begin + seq_length]
    return total.astype(jnp.bfloat16)


def long_conv(product, long_filter, skip_gain):
    seq_length = product.shape[1]
    group_size = 128

    def one_group(pieces):
        values, filters, gains = pieces
        spectrum = jnp.fft.rfft(values, n=2 * seq_length, axis=1) * jnp.fft.rfft(filters, n=2 * seq_length, axis=1)
        signal = jnp.fft.irfft(spectrum, n=2 * seq_length, axis=1)[:, :seq_length]
        return (signal + gains[:, None] * values).astype(jnp.bfloat16)

    values = product.astype(jnp.float32).reshape(-1, group_size, seq_length)
    filters = long_filter.reshape(-1, group_size, seq_length)
    gains = skip_gain.reshape(-1, group_size)
    blocks_out = lax.map(one_group, (values, filters, gains))
    return blocks_out.reshape(-1, seq_length)


def reference(inputs, streams, short_filter, long_filter, skip_gain):
    seq_length = streams.shape[2]
    mixed = lax.optimization_barrier(short_mix(streams, short_filter))
    product = (mixed[1].astype(jnp.float32) * mixed[2].astype(jnp.float32)).astype(jnp.bfloat16)
    product = lax.optimization_barrier(product)
    conv = lax.optimization_barrier(long_conv(product, long_filter, skip_gain))
    gated = (mixed[0].astype(jnp.float32) * conv.astype(jnp.float32)).astype(jnp.bfloat16)
    input_cols = inputs.astype(jnp.float32).reshape(seq_length, D // BLOCK, BLOCK)
    input_gram = jnp.einsum('tbp,tbq->pbq', input_cols, input_cols) / seq_length
    gated_rows = lax.optimization_barrier(gated).astype(jnp.float32).reshape(D // BLOCK, BLOCK, seq_length)
    output_gram = jnp.einsum('bpt,bqt->pbq', gated_rows, gated_rows) / seq_length
    return gated, input_gram, output_gram
```

```python
import math

import jax
import jax.numpy as jnp
import numpy as np
from jax import lax
from jax.experimental import pallas as pl
from jax.experimental.pallas import tpu as pltpu
from jax.sharding import PartitionSpec as P

D = 4096
BLOCK = 512
SHORT = 3
DEVICES = 128
BLOCKS = D // BLOCK
PLACES = DEVICES // BLOCKS
OWN = D // DEVICES
SIDE = 128
F32 = jnp.float32
BF16 = jnp.bfloat16
MESH = pl.DeviceIdType.MESH


def member_of(block, group):
    return 16 * block + 8 * ((group // 8 + block) % 2) + group % 8


def split(values):
    high = np.asarray(values, np.float32).astype(BF16)
    low = (values - high.astype(np.float64)).astype(np.float32).astype(BF16)
    return high, low


def tables():
    index = np.arange(SIDE)
    one = np.exp(2j * math.pi * np.outer(index + 0.25, index) / SIDE)
    turn = np.exp(2j * math.pi * np.outer(index + 0.25, index) / (SIDE * SIDE))
    two = np.exp(2j * math.pi * np.outer(index, index) / SIDE)
    order = np.array([member_of(u, j) for j in range(PLACES) for u in range(BLOCKS)])
    stacked = np.concatenate([one.real, one.imag], 0)
    high, low = split(stacked)
    one_x = np.concatenate([high[:, order], low[:, order]], 1)
    one_h = np.concatenate([high, low, high], 1)
    ahead = np.block([[two.real, two.imag], [-two.imag, two.real]])
    back = np.block([[two.real, -two.imag], [two.imag, two.real]])
    high, low = split(ahead)
    two_x = np.concatenate([high, high, low], 0)
    high, low = split(back)
    two_y = np.concatenate([high, high, low], 0)
    last = stacked.T[order] / (SIDE * SIDE)
    high, low = split(last)
    one_y = np.concatenate([high, low, high], 1)
    turn_re = np.tile(turn.real, (1, 2)).astype(np.float32)
    turn_im = np.tile(turn.imag, (1, 2)).astype(np.float32)
    edge = np.zeros((SHORT, 16, SIDE), np.float32)
    for s in range(SHORT):
        edge[s, 2 * s, SIDE - 2] = 1
        edge[s, 2 * s + 1, SIDE - 1] = 1
    return one_x, one_h, two_x, two_y, one_y, turn_re, turn_im, edge.astype(BF16)


def halves(values):
    high = values.astype(BF16)
    low = (values - high.astype(F32)).astype(BF16)
    return high, low


def dot(left, right, dims=((1,), (0,))):
    return lax.dot_general(left, right, (dims, ((), ())), preferred_element_type=F32)


def kernel(
    inputs, streams, taps, filters, gain, one_x, one_h, two_x, two_y, one_y, turn_re, turn_im, edge_at,
    gated, input_gram, output_gram,
    x_own, h_own, taps_rows, taps_cols, edge_out, edge_in,
    p_out, p_in, q_out, q_in, i_in,
    r_in, r_rows, h_rows, h_spec, y_rows, y_out, c_in,
    g_out, g_cols, part_out, part_in, fin_out, fin_in,
    local_sem, edge_sem, group_send, group_recv, block_send, block_recv, fin_send, fin_recv,
):
    me = lax.axis_index("ctx")
    block = lax.div(me, 16)
    place = lax.rem(me, 16)
    group = 8 * lax.rem(lax.div(place, 8) + block, 2) + lax.rem(place, 8)

    def member(b, j):
        return 16 * b + 8 * lax.rem(lax.div(j, 8) + b, 2) + lax.rem(j, 8)

    def remote(src, dst, send, recv, device):
        return pltpu.make_async_remote_copy(
            src_ref=src, dst_ref=dst, send_sem=send, recv_sem=recv, device_id=(device,), device_id_type=MESH
        )

    stream_copies = [
        pltpu.make_async_copy(streams.at[s], x_own.at[s], local_sem.at[s]) for s in range(SHORT)
    ]
    for copy in stream_copies:
        copy.start()
    filter_copy = pltpu.make_async_copy(filters, h_own, local_sem.at[3])
    filter_copy.start()

    def columns(u):
        return pl.ds(pl.multiple_of(u * BLOCK, BLOCK), BLOCK)

    def input_copy(u, slot):
        return remote(inputs.at[:, columns(u)], i_in.at[slot], group_send.at[2, u], group_recv.at[2, slot], member(u, group))

    own_input = pltpu.make_async_copy(inputs.at[:, columns(block)], i_in.at[block], local_sem.at[4])
    own_input.start()

    @pl.loop(1, BLOCKS)
    def _(r):
        input_copy(lax.rem(block + r, BLOCKS), block).start()

    for copy in stream_copies:
        copy.wait()
    edge = dot(edge_at[0], x_own[0], ((1,), (1,)))
    edge += dot(edge_at[1], x_own[1], ((1,), (1,)))
    edge += dot(edge_at[2], x_own[2], ((1,), (1,)))
    edge_out[...] = edge.astype(BF16)

    edge_copy = remote(edge_out, edge_in, edge_sem.at[0], edge_sem.at[1], lax.rem(me + 1, DEVICES))

    @pl.when(me < DEVICES - 1)
    def _():
        edge_copy.start()

    taps_rows[...] = jnp.zeros_like(taps_rows)
    for s in range(SHORT):
        taps_rows[SHORT * s : SHORT * s + SHORT, :] = taps[s]
    for k in range(D // SIDE):
        taps_cols[k * SIDE : (k + 1) * SIDE, :] = taps_rows[:, k * SIDE : (k + 1) * SIDE].T

    filter_copy.wait()
    for m in range(SIDE):
        h_rows[m * OWN : (m + 1) * OWN, :] = h_own[:, m * SIDE : (m + 1) * SIDE]

    @pl.when(me == 0)
    def _():
        edge_in[...] = jnp.zeros_like(edge_in)

    @pl.when(me > 0)
    def _():
        edge_copy.wait_recv()

    lane = lax.broadcasted_iota(jnp.int32, (SIDE, SIDE), 1)

    def mixed(s, row):
        row = pl.multiple_of(row, SIDE)
        here = x_own[s, pl.ds(row, SIDE), :].astype(F32)
        before = dot(edge_in[:, pl.ds(row, SIDE)], edge_at[s], ((0,), (0,)))
        one = pltpu.roll(jnp.where(lane >= SIDE - 1, before, here), 1, 1)
        two = pltpu.roll(jnp.where(lane >= SIDE - 2, before, here), 2, 1)
        col = taps_cols[pl.ds(row, SIDE), :]
        total = col[:, 3 * s : 3 * s + 1] * here
        total = total + col[:, 3 * s + 1 : 3 * s + 2] * one
        total = total + col[:, 3 * s + 2 : 3 * s + 3] * two
        return total.astype(BF16)

    def product_copy(u, slot):
        return remote(p_out.at[u], p_in.at[slot], group_send.at[0, u], group_recv.at[0, slot], member(u, group))

    def query_copy(u, slot):
        return remote(q_out.at[u], q_in.at[slot], group_send.at[1, u], group_recv.at[1, slot], member(u, group))

    def fill_product(ref, u):
        @pl.loop(0, BLOCK // SIDE)
        def _(k):
            row = u * BLOCK + k * SIDE
            value = mixed(1, row).astype(F32) * mixed(2, row).astype(F32)
            ref[pl.ds(pl.multiple_of(k * SIDE, SIDE), SIDE), :] = value.astype(BF16)

    def fill_query(ref, u):
        @pl.loop(0, BLOCK // SIDE)
        def _(k):
            ref[pl.ds(pl.multiple_of(k * SIDE, SIDE), SIDE), :] = mixed(0, u * BLOCK + k * SIDE)

    @pl.loop(1, BLOCKS)
    def _(r):
        u = lax.rem(block + r, BLOCKS)
        fill_product(p_out.at[u], u)
        product_copy(u, block).start()

    fill_product(p_in.at[block], block)

    @pl.loop(1, BLOCKS)
    def _(r):
        u = lax.rem(block + r, BLOCKS)
        fill_query(q_out.at[u], u)
        query_copy(u, block).start()

    fill_query(q_in.at[block], block)

    @pl.loop(1, BLOCKS)
    def _(r):
        u = lax.rem(block + r, BLOCKS)
        product_copy(u, u).wait_recv()

    def rows_of(o, size):
        return pl.ds(pl.multiple_of(o * size, size), size)

    def owner_copy(o, slot):
        return remote(
            p_in.at[:, rows_of(o, OWN), :], r_in.at[slot], block_send.at[0, o], block_recv.at[0, slot], 16 * block + o
        )

    @pl.loop(1, PLACES)
    def _(r):
        owner_copy(lax.rem(place + r, PLACES), group).start()

    own_product = pltpu.make_async_copy(p_in.at[:, rows_of(place, OWN), :], r_in.at[group], local_sem.at[5])
    own_product.start()

    def pair(ref, c):
        return [ref[pl.ds(c + k, SIDE, stride=OWN), :] for k in range(2)]

    def turned(values, sign):
        re, im = values[:SIDE], values[SIDE:]
        cos, sin = turn_re[...], sign * turn_im[...]
        return re * cos - im * sin, re * sin + im * cos

    def swapped(re, im):
        return jnp.concatenate(
            [jnp.concatenate([v[:, k * SIDE : (k + 1) * SIDE] for v in (re, im)], 1) for k in range(2)], 0
        )

    def three(values, axis):
        high, low = halves(values)
        return jnp.concatenate([high, low, high] if axis else [high, high, low], axis)

    @pl.loop(0, OWN // 2)
    def _(k):
        c = 2 * k
        values = jnp.concatenate(pair(h_rows, c), 1)
        first = dot(one_h[...], three(values, 0))
        spectrum = dot(three(swapped(*turned(first, 1.0)), 1), two_x[...])
        h_spec[pl.ds(pl.multiple_of(c * SIDE, 2 * SIDE), 2 * SIDE), :] = spectrum

    own_input.wait()

    @pl.loop(1, BLOCKS)
    def _(r):
        u = lax.rem(block + r, BLOCKS)
        input_copy(u, u).wait_recv()

    def part_copy(which, o, slot):
        return remote(
            part_out.at[which, rows_of(o, OWN), :],
            part_in.at[which, slot],
            block_send.at[2 + which, o],
            block_recv.at[2 + which, slot],
            16 * block + o,
        )

    def send_parts(which):
        @pl.loop(1, PLACES)
        def _(r):
            part_copy(which, lax.rem(place + r, PLACES), place).start()

        part_in[which, place] = part_out[which, rows_of(place, OWN), :]

    def sum_parts(which):
        @pl.loop(1, PLACES)
        def _(r):
            o = lax.rem(place + r, PLACES)
            part_copy(which, o, o).wait_recv()

        total = part_in[which, 0].astype(F32)
        for o in range(1, PLACES):
            total += part_in[which, o].astype(F32)
        total = total * (1.0 / (SIDE * SIDE))
        for i in range(BLOCKS):
            fin_out[which, i] = total[4 * i : 4 * i + 4]

    def fin_copy(which, i, slot, device):
        return remote(
            fin_out.at[which, i], fin_in.at[which, slot], fin_send.at[which, i], fin_recv.at[which, slot], device
        )

    def send_fin(which):
        @pl.loop(0, BLOCKS)
        def _(i):
            device = 8 * place + i

            @pl.when(device != me)
            def _():
                fin_copy(which, i, block, device).start()

            @pl.when(device == me)
            def _():
                fin_in[which, block] = fin_out[which, i]

    def wait_fin(which, out):
        @pl.loop(0, BLOCKS)
        def _(b):
            @pl.when(16 * b + lax.div(me, 8) != me)
            def _():
                fin_copy(which, 0, b, me).wait_recv()

        for r in range(4):
            out[r] = fin_in[which, :, r, :]

    rows = i_in[...].reshape(BLOCKS * SIDE, BLOCK)
    part_out[0] = dot(rows, rows, ((0,), (0,))).astype(BF16)
    send_parts(0)

    @pl.loop(1, PLACES)
    def _(r):
        j = lax.rem(group + r, PLACES)
        owner_copy(place, j).wait_recv()

    own_product.wait()

    @pl.loop(0, SIDE)
    def _(k):
        r_rows[rows_of(k, OWN), :] = r_in[lax.div(k, BLOCKS), lax.rem(k, BLOCKS)].astype(F32)

    @pl.loop(0, OWN // 2)
    def _(k):
        c = 2 * k
        values = pair(r_rows, c)
        exact = jnp.concatenate(values, 1).astype(BF16)
        first = dot(one_x[...], jnp.concatenate([exact, exact], 0))
        spectrum = dot(three(swapped(*turned(first, 1.0)), 1), two_x[...])
        other = h_spec[pl.ds(pl.multiple_of(c * SIDE, 2 * SIDE), 2 * SIDE), :]
        x_re, x_im, h_re, h_im = spectrum[:, :SIDE], spectrum[:, SIDE:], other[:, :SIDE], other[:, SIDE:]
        both = jnp.concatenate([x_re * h_re - x_im * h_im, x_re * h_im + x_im * h_re], 1)
        back = dot(three(both, 1), two_y[...])
        lanes = jnp.concatenate(
            [jnp.concatenate([back[q * SIDE : (q + 1) * SIDE, p * SIDE : (p + 1) * SIDE] for q in range(2)], 1) for p in range(2)],
            0,
        )
        signal = dot(one_y[...], three(jnp.concatenate(turned(lanes, -1.0), 0), 0))
        for q in range(2):
            y_rows[pl.ds(c + q, SIDE, stride=OWN), :] = signal[:, q * SIDE : (q + 1) * SIDE] + gain[c + q] * values[q]

    def conv_copy(j, slot):
        return remote(
            y_out.at[j], c_in.at[slot], block_send.at[1, j], block_recv.at[1, slot], member(block, j)
        )

    @pl.loop(0, PLACES)
    def _(r):
        j = lax.rem(group + 1 + r, PLACES)
        for u in range(BLOCKS):
            y_out[j, u] = y_rows[rows_of(j * BLOCKS + u, OWN), :].astype(BF16)

        @pl.when(r < PLACES - 1)
        def _():
            conv_copy(j, place).start()

    c_in[place] = y_out[group]
    sum_parts(0)
    send_fin(0)

    @pl.loop(1, BLOCKS)
    def _(r):
        u = lax.rem(block + r, BLOCKS)
        query_copy(u, u).wait_recv()

    @pl.loop(1, PLACES)
    def _(r):
        o = lax.rem(place + r, PLACES)
        conv_copy(group, o).wait_recv()

    def gated_copy(u, slot):
        return remote(
            g_out.at[u], gated.at[columns(slot), :], group_send.at[3, u], group_recv.at[3, slot], member(u, group)
        )

    def fill_gated(u):
        conv = c_in[:, u].reshape(BLOCK, SIDE).astype(F32)
        value = (q_in[u].astype(F32) * conv).astype(BF16)
        g_out[u] = value
        g_cols[:, pl.ds(pl.multiple_of(u * SIDE, SIDE), SIDE)] = value

    @pl.loop(1, BLOCKS)
    def _(r):
        u = lax.rem(block + r, BLOCKS)
        fill_gated(u)
        gated_copy(u, block).start()

    fill_gated(block)
    own_gated = pltpu.make_async_copy(g_out.at[block], gated.at[columns(block), :], local_sem.at[6])
    own_gated.start()

    part_out[1] = dot(g_cols[...], g_cols[...], ((1,), (1,))).astype(BF16)
    send_parts(1)
    wait_fin(0, input_gram)
    sum_parts(1)
    send_fin(1)
    wait_fin(1, output_gram)

    own_gated.wait()

    @pl.loop(1, BLOCKS)
    def _(r):
        u = lax.rem(block + r, BLOCKS)
        gated_copy(u, u).wait_recv()
        product_copy(u, u).wait_send()
        query_copy(u, u).wait_send()
        input_copy(u, u).wait_send()
        gated_copy(u, u).wait_send()

    @pl.loop(1, PLACES)
    def _(r):
        o = lax.rem(place + r, PLACES)
        owner_copy(o, o).wait_send()
        part_copy(0, o, o).wait_send()
        part_copy(1, o, o).wait_send()
        conv_copy(lax.rem(group + r, PLACES), o).wait_send()

    @pl.loop(0, BLOCKS)
    def _(i):
        @pl.when(8 * place + i != me)
        def _():
            fin_copy(0, i, i, me).wait_send()
            fin_copy(1, i, i, me).wait_send()

    @pl.when(me < DEVICES - 1)
    def _():
        edge_copy.wait_send()


def body(inputs, streams, short_filter, long_filter, skip_gain):
    anywhere = pl.BlockSpec(memory_space=pl.ANY)
    vmem = pl.BlockSpec(memory_space=pltpu.VMEM)
    smem = pl.BlockSpec(memory_space=pltpu.SMEM)
    constants = tables()
    dma = pltpu.SemaphoreType.DMA
    gram = jax.ShapeDtypeStruct((BLOCK // DEVICES, BLOCKS, BLOCK), F32)
    return pl.pallas_call(
        kernel,
        out_shape=(jax.ShapeDtypeStruct((D, SIDE), BF16), gram, gram),
        in_specs=[anywhere, anywhere, vmem, anywhere, smem] + [vmem] * len(constants),
        out_specs=(anywhere, vmem, vmem),
        scratch_shapes=[
            pltpu.VMEM((SHORT, D, SIDE), BF16),
            pltpu.VMEM((OWN, SIDE * SIDE), F32),
            pltpu.VMEM((16, D), F32),
            pltpu.VMEM((D, 16), F32),
            pltpu.VMEM((16, D), BF16),
            pltpu.VMEM((16, D), BF16),
            pltpu.VMEM((BLOCKS, BLOCK, SIDE), BF16),
            pltpu.VMEM((BLOCKS, BLOCK, SIDE), BF16),
            pltpu.VMEM((BLOCKS, BLOCK, SIDE), BF16),
            pltpu.VMEM((BLOCKS, BLOCK, SIDE), BF16),
            pltpu.VMEM((BLOCKS, SIDE, BLOCK), BF16),
            pltpu.VMEM((PLACES, BLOCKS, OWN, SIDE), BF16),
            pltpu.VMEM((SIDE * OWN, SIDE), F32),
            pltpu.VMEM((SIDE * OWN, SIDE), F32),
            pltpu.VMEM((OWN * SIDE, 2 * SIDE), F32),
            pltpu.VMEM((SIDE * OWN, SIDE), F32),
            pltpu.VMEM((PLACES, BLOCKS, OWN, SIDE), BF16),
            pltpu.VMEM((PLACES, BLOCKS, OWN, SIDE), BF16),
            pltpu.VMEM((BLOCKS, BLOCK, SIDE), BF16),
            pltpu.VMEM((BLOCK, BLOCKS * SIDE), BF16),
            pltpu.VMEM((2, BLOCK, BLOCK), BF16),
            pltpu.VMEM((2, PLACES, OWN, BLOCK), BF16),
            pltpu.VMEM((2, BLOCKS, 4, BLOCK), F32),
            pltpu.VMEM((2, BLOCKS, 4, BLOCK), F32),
            dma((8,)),
            dma((2,)),
            dma((4, BLOCKS)),
            dma((4, BLOCKS)),
            dma((4, PLACES)),
            dma((4, PLACES)),
            dma((2, BLOCKS)),
            dma((2, BLOCKS)),
        ],
        compiler_params=pltpu.CompilerParams(has_side_effects=True, vmem_limit_bytes=56 * 1024 * 1024),
    )(inputs, streams, short_filter, long_filter, skip_gain, *[jnp.asarray(c) for c in constants])


def solution(mesh):
    in_specs = (P("ctx", None), P(None, None, "ctx"), P(), P("ctx", None), P("ctx"))
    out_specs = (P(None, "ctx"), P("ctx", None, None), P("ctx", None, None))
    return jax.shard_map(body, mesh=mesh, in_specs=in_specs, out_specs=out_specs, check_vma=False)
```

```python
import math

import jax
import jax.numpy as jnp
import numpy as np
from jax import lax
from jax.experimental import pallas as pl
from jax.experimental.pallas import tpu as pltpu
from jax.sharding import PartitionSpec as P

D = 4096
BLOCK = 512
SHORT = 3
DEVICES = 128
BLOCKS = D // BLOCK
PLACES = DEVICES // BLOCKS
OWN = D // DEVICES
HALF = OWN // 2
SIDE = 128
PAIRS = 2
EARLY = 4
F32 = jnp.float32
BF16 = jnp.bfloat16
MESH = pl.DeviceIdType.MESH


def member_of(block, group):
    return 16 * block + 8 * ((group // 8 + block) % 2) + group % 8


def split(values):
    high = np.asarray(values, np.float32).astype(BF16)
    low = (values - high.astype(np.float64)).astype(np.float32).astype(BF16)
    return high, low


def tables():
    index = np.arange(SIDE)
    one = np.exp(2j * math.pi * np.outer(index + 0.25, index) / SIDE)
    turn = np.exp(2j * math.pi * np.outer(index + 0.25, index) / (SIDE * SIDE))
    two = np.exp(2j * math.pi * np.outer(index, index) / SIDE)
    order = np.array([member_of(u, j) for j in range(PLACES) for u in range(BLOCKS)])
    stacked = np.concatenate([one.real, one.imag], 0)
    high, low = split(stacked)
    one_x = np.concatenate([high[:, order], low[:, order]], 1)
    one_h = np.concatenate([high, low, high], 1)
    ahead = np.block([[two.real, two.imag], [-two.imag, two.real]])
    back = np.block([[two.real, -two.imag], [two.imag, two.real]])
    high, low = split(ahead)
    two_x = np.concatenate([high, high, low], 0)
    high, low = split(back)
    two_y = np.concatenate([high, high, low], 0)
    last = stacked.T[order] / (SIDE * SIDE)
    high, low = split(last)
    one_y = np.concatenate([high, low, high], 1)
    turn_re = np.tile(turn.real, (1, 2)).astype(np.float32)
    turn_im = np.tile(turn.imag, (1, 2)).astype(np.float32)
    pick = np.zeros((2, 2 * SIDE, SIDE), np.float32)
    pick[0, SIDE - 2, 0] = pick[0, SIDE - 1, 1] = pick[0, 2 * SIDE - 2, 2] = pick[0, 2 * SIDE - 1, 3] = 1
    pick[1, SIDE - 2, 0] = pick[1, SIDE - 1, 1] = 1
    shift = np.zeros((SHORT, 2 * SIDE, 2 * SIDE), np.float32)
    for s in range(SHORT):
        at = SIDE + (2 if s == 2 else 0)
        shift[s, index[:-1], index[1:]] = 1
        shift[s, index[:-2], SIDE + index[2:]] = 1
        shift[s, at + 1, 0] = shift[s, at, SIDE] = shift[s, at + 1, SIDE + 1] = 1
    return one_x, one_h, two_x, two_y, one_y, turn_re, turn_im, pick.astype(BF16), shift.astype(BF16)


def halves(values):
    high = values.astype(BF16)
    low = (values - high.astype(F32)).astype(BF16)
    return high, low


def three(values, axis):
    high, low = halves(values)
    return jnp.concatenate([high, low, high] if axis else [high, high, low], axis)


def dot(left, right, dims=((1,), (0,))):
    return lax.dot_general(left, right, (dims, ((), ())), preferred_element_type=F32)


def kernel(
    inputs, streams, taps, filters, gain, one_x, one_h, two_x, two_y, one_y, turn_re, turn_im, pick, shift,
    gated, sums,
    x_own, h_own, taps_rows, taps_cols, edge_out, edge_in, edge_wide,
    p_out, p_in, q_out, q_in, i_in,
    r_in, r_rows, h_rows, h_spec, y_rows, y_out, c_in,
    g_out, g_cols, part_out, part_in, fin_out,
    local_sem, edge_sem, group_send, group_recv, block_send, block_recv, fin_send, fin_recv,
):
    me = lax.axis_index("ctx")
    block = lax.div(me, 16)
    place = lax.rem(me, 16)
    group = 8 * lax.rem(lax.div(place, 8) + block, 2) + lax.rem(place, 8)

    def member(b, j):
        return 16 * b + 8 * lax.rem(lax.div(j, 8) + b, 2) + lax.rem(j, 8)

    def remote(src, dst, send, recv, device):
        return pltpu.make_async_remote_copy(
            src_ref=src, dst_ref=dst, send_sem=send, recv_sem=recv, device_id=(device,), device_id_type=MESH
        )

    def other_blocks(first=1, last=BLOCKS):
        def loop(step):
            pl.loop(first, last)(lambda r: step(lax.rem(block + r, BLOCKS)))

        return loop

    def other_places(step):
        pl.loop(1, PLACES)(lambda r: step(lax.rem(place + r, PLACES)))

    def other_groups(step):
        pl.loop(1, PLACES)(lambda r: step(lax.rem(group + r, PLACES)))

    barrier = pltpu.get_barrier_semaphore()

    def greet(device):
        pl.semaphore_signal(barrier, inc=1, device_id=(device,), device_id_type=MESH)

    other_blocks()(lambda u: greet(member(u, group)))
    other_places(lambda o: greet(16 * block + o))
    greet(lax.rem(me + 1, DEVICES))
    greet(lax.rem(me + DEVICES - 1, DEVICES))

    @pl.loop(0, BLOCKS)
    def _(i):
        @pl.when(8 * place + i != me)
        def _():
            greet(8 * place + i)

        @pl.when(16 * i + lax.div(me, 8) != me)
        def _():
            greet(16 * i + lax.div(me, 8))

    stream_copies = [
        pltpu.make_async_copy(streams.at[s], x_own.at[s], local_sem.at[s]) for s in range(SHORT)
    ]
    for s in (1, 2, 0):
        stream_copies[s].start()
    filter_copy = pltpu.make_async_copy(filters, h_own, local_sem.at[3])
    filter_copy.start()

    taps_rows[...] = jnp.zeros_like(taps_rows)
    for s in range(SHORT):
        taps_rows[SHORT * s : SHORT * s + SHORT, :] = taps[s]
    for k in range(D // SIDE):
        cols = taps_rows[:, k * SIDE : (k + 1) * SIDE].T
        taps_cols[k // 4, 4 * (k % 4) : 4 * (k % 4) + 4] = cols.reshape(4, 2, HALF, 16)

    def edge_copy(which):
        return remote(
            edge_out.at[which], edge_in.at[which], edge_sem.at[0, which], edge_sem.at[1, which], lax.rem(me + 1, DEVICES)
        )

    def eight(s, u, h, k):
        return x_own[s, u, 8 * k : 8 * k + 8, h].reshape(SIDE, SIDE)

    def fill_edge(which, width):
        edge = jnp.zeros((SIDE, SIDE), F32)
        for u in range(BLOCKS):
            for h in range(2):
                for k in range(2):
                    if which == 0:
                        got = dot(jnp.concatenate([eight(1, u, h, k), eight(2, u, h, k)], 1), pick[0])
                    else:
                        got = dot(eight(0, u, h, k), pick[1, :SIDE])
                    at = width * (4 * u + 2 * h + k)
                    edge += pltpu.roll(got, at, 1) if at else got
        edge_out[which] = edge.astype(BF16)

    stream_copies[1].wait()
    stream_copies[2].wait()
    fill_edge(0, 4)

    pl.semaphore_wait(barrier, 2 + BLOCKS - 1 + PLACES - 1 + 2 * BLOCKS - 2 * jnp.where(lax.div(me, 8) == place, 1, 0))

    @pl.when(me < DEVICES - 1)
    def _():
        edge_copy(0).start()

    def columns(u):
        return pl.ds(pl.multiple_of(u * BLOCK, BLOCK), BLOCK)

    def input_copy(u, slot):
        return remote(inputs.at[:, columns(u)], i_in.at[slot], group_send.at[2, u], group_recv.at[2, slot], member(u, group))

    own_input = pltpu.make_async_copy(inputs.at[:, columns(block)], i_in.at[block], local_sem.at[4])
    own_input.start()
    other_blocks(1, EARLY)(lambda u: input_copy(u, block).start())

    stream_copies[0].wait()
    fill_edge(1, 2)

    @pl.when(me < DEVICES - 1)
    def _():
        edge_copy(1).start()

    filter_copy.wait()
    for m in range(SIDE):
        h_rows[m * OWN : (m + 1) * OWN, :] = h_own[:, m * SIDE : (m + 1) * SIDE]

    def take_edge(which):
        @pl.when(me == 0)
        def _():
            edge_in[which] = jnp.zeros((SIDE, SIDE), BF16)

        @pl.when(me > 0)
        def _():
            edge_copy(which).wait_recv()

        edge_wide[which] = edge_in[which].astype(F32)

    def mixed(s, u, h, k, edge):
        here = eight(s, u, h, k)
        moved = dot(jnp.concatenate([here, edge], 1), shift[s])
        col = taps_cols[u, 8 * k : 8 * k + 8, h].reshape(SIDE, 16)
        total = col[:, 3 * s : 3 * s + 1] * here.astype(F32)
        total = total + col[:, 3 * s + 1 : 3 * s + 2] * moved[:, :SIDE]
        total = total + col[:, 3 * s + 2 : 3 * s + 3] * moved[:, SIDE:]
        return total.astype(BF16)

    def edge_of(which, width, u, h, k):
        at = lax.rem(SIDE - width * (4 * u + 2 * h + k), SIDE)
        return pltpu.roll(edge_wide[which], at, 1).astype(BF16)

    def product_copy(u, slot, h):
        return remote(p_out.at[u, h], p_in.at[slot, h], group_send.at[h, u], group_recv.at[h, slot], member(u, group))

    def query_copy(u, slot):
        return remote(q_out.at[u], q_in.at[slot], group_send.at[3, u], group_recv.at[3, slot], member(u, group))

    def fill_product(ref, u, h):
        for k in range(2):
            edge = edge_of(0, 4, u, h, k)
            value = mixed(1, u, h, k, edge).astype(F32) * mixed(2, u, h, k, edge).astype(F32)
            ref[8 * k : 8 * k + 8] = value.astype(BF16).reshape(8, HALF, SIDE)

    def fill_query(ref, u):
        for h in range(2):
            for k in range(2):
                value = mixed(0, u, h, k, edge_of(1, 2, u, h, k))
                ref[h, 8 * k : 8 * k + 8] = value.reshape(8, HALF, SIDE)

    take_edge(0)

    for h in range(2):
        @other_blocks()
        def _(u):
            fill_product(p_out.at[u, h], u, h)
            product_copy(u, block, h).start()

        fill_product(p_in.at[block, h], block, h)

    take_edge(1)

    @other_blocks()
    def _(u):
        fill_query(q_out.at[u], u)
        query_copy(u, block).start()

    fill_query(q_in.at[block], block)
    other_blocks(EARLY)(lambda u: input_copy(u, block).start())

    def pair(ref, c, stride):
        return [ref[pl.ds(c + k, SIDE, stride=stride), :] for k in range(2)]

    def turned(values, sign):
        re, im = values[:SIDE], values[SIDE:]
        cos, sin = turn_re[...], sign * turn_im[...]
        return re * cos - im * sin, re * sin + im * cos

    def swapped(re, im):
        return jnp.concatenate(
            [jnp.concatenate([v[:, k * SIDE : (k + 1) * SIDE] for v in (re, im)], 1) for k in range(2)], 0
        )

    def spectrum_rows(c):
        return pl.ds(pl.multiple_of(c * SIDE, 2 * SIDE), 2 * SIDE)

    def filter_half(h):
        @pl.loop(0, HALF // (2 * PAIRS))
        def _(step):
            starts = [h * HALF + 2 * (PAIRS * step + q) for q in range(PAIRS)]
            values = [jnp.concatenate(pair(h_rows, c, OWN), 1) for c in starts]
            first = [dot(one_h[...], three(v, 0)) for v in values]
            second = [dot(three(swapped(*turned(v, 1.0)), 1), two_x[...]) for v in first]
            for c, v in zip(starts, second):
                h_spec[spectrum_rows(c), :] = v

    def owner_copy(o, slot, h):
        return remote(
            p_in.at[:, h, o], r_in.at[h, slot], block_send.at[h, o], block_recv.at[h, slot], 16 * block + o
        )

    def own_product(h):
        return pltpu.make_async_copy(p_in.at[:, h, place], r_in.at[h, group], local_sem.at[5 + h])

    def forward(h):
        other_blocks()(lambda u: product_copy(u, u, h).wait_recv())
        other_places(lambda o: owner_copy(o, group, h).start())
        own_product(h).start()

    def conv_copy(j, slot, h):
        return remote(
            y_out.at[h, j], c_in.at[h, slot], block_send.at[2 + h, j], block_recv.at[2 + h, slot], member(block, j)
        )

    def convolve(h):
        other_groups(lambda j: owner_copy(place, j, h).wait_recv())
        own_product(h).wait()

        @pl.loop(0, PLACES)
        def _(j):
            for u in range(BLOCKS):
                at = pl.multiple_of((j * BLOCKS + u) * HALF, HALF)
                r_rows[pl.ds(at, HALF), :] = r_in[h, j, u].astype(F32)

        @pl.loop(0, HALF // (2 * PAIRS))
        def _(step):
            starts = [2 * (PAIRS * step + q) for q in range(PAIRS)]
            values = [pair(r_rows, c, HALF) for c in starts]
            exact = [jnp.concatenate(v, 1).astype(BF16) for v in values]
            first = [dot(one_x[...], jnp.concatenate([v, v], 0)) for v in exact]
            second = [dot(three(swapped(*turned(v, 1.0)), 1), two_x[...]) for v in first]
            third = []
            for c, v in zip(starts, second):
                other = h_spec[spectrum_rows(h * HALF + c), :]
                x_re, x_im, h_re, h_im = v[:, :SIDE], v[:, SIDE:], other[:, :SIDE], other[:, SIDE:]
                third.append(jnp.concatenate([x_re * h_re - x_im * h_im, x_re * h_im + x_im * h_re], 1))
            third = [dot(three(v, 1), two_y[...]) for v in third]
            third = [
                jnp.concatenate(
                    [
                        jnp.concatenate([v[q * SIDE : (q + 1) * SIDE, p * SIDE : (p + 1) * SIDE] for q in range(2)], 1)
                        for p in range(2)
                    ],
                    0,
                )
                for v in third
            ]
            signal = [dot(one_y[...], three(jnp.concatenate(turned(v, -1.0), 0), 0)) for v in third]
            for c, v, w in zip(starts, values, signal):
                for q in range(2):
                    y_rows[pl.ds(c + q, SIDE, stride=HALF), :] = (
                        w[:, q * SIDE : (q + 1) * SIDE] + gain[h * HALF + c + q] * v[q]
                    )

        def fill_conv(ref, j):
            for u in range(BLOCKS):
                at = pl.multiple_of((j * BLOCKS + u) * HALF, HALF)
                ref[u] = y_rows[pl.ds(at, HALF), :].astype(BF16)

        @other_groups
        def _(j):
            fill_conv(y_out.at[h, j], j)
            conv_copy(j, place, h).start()

        fill_conv(c_in.at[h, place], group)

    def part_rows(o):
        return pl.ds(pl.multiple_of(o * OWN, OWN), OWN)

    def part_copy(which, o, slot):
        return remote(
            part_out.at[which, part_rows(o), :],
            part_in.at[which, slot],
            block_send.at[4 + which, o],
            block_recv.at[4 + which, slot],
            16 * block + o,
        )

    def send_parts(which):
        other_places(lambda o: part_copy(which, o, place).start())
        part_in[which, place] = part_out[which, part_rows(place), :]

    def fin_copy(which, i, slot, device):
        return remote(
            fin_out.at[which, i], sums.at[which, slot], fin_send.at[which, i], fin_recv.at[which, slot], device
        )

    def sum_parts(which):
        other_places(lambda o: part_copy(which, o, o).wait_recv())
        total = part_in[which, 0].astype(F32)
        for o in range(1, PLACES):
            total += part_in[which, o].astype(F32)
        total = total * (1.0 / (SIDE * SIDE))
        for i in range(BLOCKS):
            fin_out[which, i] = total[4 * i : 4 * i + 4]

        @pl.loop(0, BLOCKS)
        def _(i):
            device = 8 * place + i

            @pl.when(device != me)
            def _():
                fin_copy(which, i, block, device).start()

            @pl.when(device == me)
            def _():
                sums[which, block] = fin_out[which, i]

    def wait_fin(which):
        @pl.loop(0, BLOCKS)
        def _(b):
            @pl.when(16 * b + lax.div(me, 8) != me)
            def _():
                fin_copy(which, 0, b, me).wait_recv()

    filter_half(0)
    forward(0)
    filter_half(1)
    forward(1)
    convolve(0)
    convolve(1)

    own_input.wait()
    other_blocks()(lambda u: input_copy(u, u).wait_recv())
    rows = i_in[...].reshape(BLOCKS * SIDE, BLOCK)
    part_out[0] = dot(rows, rows, ((0,), (0,))).astype(BF16)
    send_parts(0)

    def gated_copy(u, slot, h):
        return remote(
            g_out.at[u, h], gated.at[slot, :, h], group_send.at[4 + h, u], group_recv.at[4 + h, slot], member(u, group)
        )

    def own_gated(h):
        return pltpu.make_async_copy(g_out.at[block, h], gated.at[block, :, h], local_sem.at[7 + h])

    def fill_gated(u, h):
        value = (q_in[u, h].astype(F32) * c_in[h, :, u].astype(F32)).astype(BF16)
        g_out[u, h] = value
        g_cols[:, h, :, pl.ds(pl.multiple_of(u * SIDE, SIDE), SIDE)] = value

    other_blocks()(lambda u: query_copy(u, u).wait_recv())

    for h in range(2):
        other_places(lambda o: conv_copy(group, o, h).wait_recv())

        @other_blocks()
        def _(u):
            fill_gated(u, h)
            gated_copy(u, block, h).start()

        fill_gated(block, h)
        own_gated(h).start()

    columns_all = g_cols[...].reshape(BLOCK, BLOCKS * SIDE)
    part_out[1] = dot(columns_all, columns_all, ((1,), (1,))).astype(BF16)
    send_parts(1)
    sum_parts(0)
    sum_parts(1)
    wait_fin(0)
    wait_fin(1)

    for h in range(2):
        own_gated(h).wait()

    @other_blocks()
    def _(u):
        for h in range(2):
            gated_copy(u, u, h).wait_recv()
            gated_copy(u, u, h).wait_send()
            product_copy(u, u, h).wait_send()
        query_copy(u, u).wait_send()
        input_copy(u, u).wait_send()

    @other_places
    def _(o):
        for h in range(2):
            owner_copy(o, o, h).wait_send()
            part_copy(h, o, o).wait_send()

    @other_groups
    def _(j):
        for h in range(2):
            conv_copy(j, j, h).wait_send()

    @pl.loop(0, BLOCKS)
    def _(i):
        @pl.when(8 * place + i != me)
        def _():
            for which in range(2):
                fin_copy(which, i, i, me).wait_send()

    @pl.when(me < DEVICES - 1)
    def _():
        for which in range(2):
            edge_copy(which).wait_send()


def write_kernel(got, sums, gated, input_gram, output_gram, held, sems):
    def taken(b):
        return pltpu.make_async_copy(got.at[b], held.at[b], sems.at[0, b])

    def given(b):
        return pltpu.make_async_copy(held.at[b], gated.at[b], sems.at[1, b])

    for b in range(BLOCKS):
        taken(b).start()
    for r in range(BLOCK // DEVICES):
        input_gram[r] = sums[0, :, r, :]
        output_gram[r] = sums[1, :, r, :]
    for b in range(BLOCKS):
        taken(b).wait()
        given(b).start()
    for b in range(BLOCKS):
        given(b).wait()


def body(inputs, streams, short_filter, long_filter, skip_gain):
    anywhere = pl.BlockSpec(memory_space=pl.ANY)
    vmem = pl.BlockSpec(memory_space=pltpu.VMEM)
    smem = pl.BlockSpec(memory_space=pltpu.SMEM)
    constants = tables()
    dma = pltpu.SemaphoreType.DMA
    rows = BLOCK // DEVICES
    split_streams = streams.reshape(SHORT, BLOCKS, PLACES, 2, HALF, SIDE)
    got, sums = pl.pallas_call(
        kernel,
        out_shape=(
            jax.ShapeDtypeStruct((BLOCKS, PLACES, 2, HALF, SIDE), BF16),
            jax.ShapeDtypeStruct((2, BLOCKS, rows, BLOCK), F32),
        ),
        in_specs=[anywhere, anywhere, vmem, anywhere, smem] + [vmem] * len(constants),
        out_specs=(anywhere, vmem),
        scratch_shapes=[
            pltpu.VMEM((SHORT, BLOCKS, PLACES, 2, HALF, SIDE), BF16),
            pltpu.VMEM((OWN, SIDE * SIDE), F32),
            pltpu.VMEM((16, D), F32),
            pltpu.VMEM((BLOCKS, PLACES, 2, HALF, 16), F32),
            pltpu.VMEM((2, SIDE, SIDE), BF16),
            pltpu.VMEM((2, SIDE, SIDE), BF16),
            pltpu.VMEM((2, SIDE, SIDE), F32),
            pltpu.VMEM((BLOCKS, 2, PLACES, HALF, SIDE), BF16),
            pltpu.VMEM((BLOCKS, 2, PLACES, HALF, SIDE), BF16),
            pltpu.VMEM((BLOCKS, 2, PLACES, HALF, SIDE), BF16),
            pltpu.VMEM((BLOCKS, 2, PLACES, HALF, SIDE), BF16),
            pltpu.VMEM((BLOCKS, SIDE, BLOCK), BF16),
            pltpu.VMEM((2, PLACES, BLOCKS, HALF, SIDE), BF16),
            pltpu.VMEM((SIDE * HALF, SIDE), F32),
            pltpu.VMEM((SIDE * OWN, SIDE), F32),
            pltpu.VMEM((OWN * SIDE, 2 * SIDE), F32),
            pltpu.VMEM((SIDE * HALF, SIDE), F32),
            pltpu.VMEM((2, PLACES, BLOCKS, HALF, SIDE), BF16),
            pltpu.VMEM((2, PLACES, BLOCKS, HALF, SIDE), BF16),
            pltpu.VMEM((BLOCKS, 2, PLACES, HALF, SIDE), BF16),
            pltpu.VMEM((PLACES, 2, HALF, BLOCKS * SIDE), BF16),
            pltpu.VMEM((2, BLOCK, BLOCK), BF16),
            pltpu.VMEM((2, PLACES, OWN, BLOCK), BF16),
            pltpu.VMEM((2, BLOCKS, rows, BLOCK), F32),
            dma((9,)),
            dma((2, 2)),
            dma((6, BLOCKS)),
            dma((6, BLOCKS)),
            dma((6, PLACES)),
            dma((6, PLACES)),
            dma((2, BLOCKS)),
            dma((2, BLOCKS)),
        ],
        compiler_params=pltpu.CompilerParams(
            collective_id=0, has_side_effects=True, vmem_limit_bytes=56 * 1024 * 1024
        ),
    )(inputs, split_streams, short_filter, long_filter, skip_gain, *[jnp.asarray(c) for c in constants])
    gram = jax.ShapeDtypeStruct((rows, BLOCKS, BLOCK), F32)
    gated, input_gram, output_gram = pl.pallas_call(
        write_kernel,
        out_shape=(jax.ShapeDtypeStruct((BLOCKS, PLACES, 2, HALF, SIDE), BF16), gram, gram),
        in_specs=[anywhere, vmem],
        out_specs=(anywhere, vmem, vmem),
        scratch_shapes=[pltpu.VMEM((BLOCKS, PLACES, 2, HALF, SIDE), BF16), dma((2, BLOCKS))],
    )(got, sums)
    return gated.reshape(D, SIDE), input_gram, output_gram


def solution(mesh):
    in_specs = (P("ctx", None), P(None, None, "ctx"), P(), P("ctx", None), P("ctx"))
    out_specs = (P(None, "ctx"), P("ctx", None, None), P("ctx", None, None))
    return jax.shard_map(body, mesh=mesh, in_specs=in_specs, out_specs=out_specs, check_vma=False)
```

```python
import math

import jax
import jax.numpy as jnp
import numpy as np
from jax import lax
from jax.experimental import pallas as pl
from jax.experimental.pallas import tpu as pltpu
from jax.sharding import PartitionSpec as P

D = 4096
BLOCK = 512
SHORT = 3
DEVICES = 128
BLOCKS = D // BLOCK
PLACES = DEVICES // BLOCKS
OWN = D // DEVICES
HALF = OWN // 2
SIDE = 128
PAIRS = 2
CONSTANTS = 9
F32 = jnp.float32
BF16 = jnp.bfloat16
MESH = pl.DeviceIdType.MESH


def member_of(block, group):
    return 16 * block + 8 * ((group // 8 + block) % 2) + group % 8


def split(values):
    high = np.asarray(values, np.float32).astype(BF16)
    low = (values - high.astype(np.float64)).astype(np.float32).astype(BF16)
    return high, low


def tables():
    index = np.arange(SIDE)
    one = np.exp(2j * math.pi * np.outer(index + 0.25, index) / SIDE)
    turn = np.exp(2j * math.pi * np.outer(index + 0.25, index) / (SIDE * SIDE))
    two = np.exp(2j * math.pi * np.outer(index, index) / SIDE)
    order = np.array([member_of(u, j) for j in range(PLACES) for u in range(BLOCKS)])
    stacked = np.concatenate([one.real, one.imag], 0)
    high, low = split(stacked)
    one_x = np.concatenate([high[:, order], low[:, order]], 1)
    one_h = np.concatenate([high, low, high], 1)
    ahead = np.block([[two.real, two.imag], [-two.imag, two.real]])
    back = np.block([[two.real, -two.imag], [two.imag, two.real]])
    high, low = split(ahead)
    two_x = np.concatenate([high, high, low], 0)
    high, low = split(back)
    two_y = np.concatenate([high, high, low], 0)
    last = stacked.T[order] / (SIDE * SIDE)
    high, low = split(last)
    one_y = np.concatenate([high, low, high], 1)
    turn_re = np.tile(turn.real, (1, 2)).astype(np.float32)
    turn_im = np.tile(turn.imag, (1, 2)).astype(np.float32)
    pick = np.zeros((2, 2 * SIDE, SIDE), np.float32)
    pick[0, SIDE - 2, 0] = pick[0, SIDE - 1, 1] = pick[0, 2 * SIDE - 2, 2] = pick[0, 2 * SIDE - 1, 3] = 1
    pick[1, SIDE - 2, 0] = pick[1, SIDE - 1, 1] = 1
    shift = np.zeros((SHORT, 2 * SIDE, 2 * SIDE), np.float32)
    for s in range(SHORT):
        at = SIDE + (2 if s == 2 else 0)
        shift[s, index[:-1], index[1:]] = 1
        shift[s, index[:-2], SIDE + index[2:]] = 1
        shift[s, at + 1, 0] = shift[s, at, SIDE] = shift[s, at + 1, SIDE + 1] = 1
    return one_x, one_h, two_x, two_y, one_y, turn_re, turn_im, pick.astype(BF16), shift.astype(BF16)


def halves(values):
    high = values.astype(BF16)
    low = (values - high.astype(F32)).astype(BF16)
    return high, low


def three(values, axis):
    high, low = halves(values)
    return jnp.concatenate([high, low, high] if axis else [high, high, low], axis)


def dot(left, right, dims=((1,), (0,))):
    return lax.dot_general(left, right, (dims, ((), ())), preferred_element_type=F32)


def kernel(
    inputs, streams, taps, filters, gain, *rest
):
    constants, rest = rest[:CONSTANTS], rest[CONSTANTS:]
    local, rest = rest[-CONSTANTS:], rest[:-CONSTANTS]
    one_x, one_h, two_x, two_y, one_y, turn_re, turn_im, pick, shift = local
    (gated, sums,
    x_own, h_own, taps_rows, taps_cols, edge_out, edge_in, edge_wide,
    p_out, p_in, q_out, q_in, i_in,
    r_in, r_rows, h_rows, h_spec, y_rows, y_out, c_in,
    g_out, g_cols, part_out, part_in, fin_out,
    local_sem, edge_sem, group_send, group_recv, block_send, block_recv, fin_send, fin_recv, constant_sem) = rest
    me = lax.axis_index("ctx")
    block = lax.div(me, 16)
    place = lax.rem(me, 16)
    group = 8 * lax.rem(lax.div(place, 8) + block, 2) + lax.rem(place, 8)
    line, spot = lax.div(me, 8), lax.rem(me, 8)

    def member(b, j):
        return 16 * b + 8 * lax.rem(lax.div(j, 8) + b, 2) + lax.rem(j, 8)

    def remote(src, dst, send, recv, device):
        return pltpu.make_async_remote_copy(
            src_ref=src, dst_ref=dst, send_sem=send, recv_sem=recv, device_id=(device,), device_id_type=MESH
        )

    def other_blocks(step):
        pl.loop(1, BLOCKS)(lambda r: step(lax.rem(block + r, BLOCKS)))

    def other_places(step):
        pl.loop(1, PLACES)(lambda r: step(lax.rem(place + r, PLACES)))

    def other_groups(step):
        pl.loop(1, PLACES)(lambda r: step(lax.rem(group + r, PLACES)))

    def other_lines(step):
        pl.loop(1, PLACES)(lambda r: step(lax.rem(line + r, PLACES)))

    def other_spots(step):
        pl.loop(1, BLOCKS)(lambda r: step(lax.rem(spot + r, BLOCKS)))

    barrier = pltpu.get_barrier_semaphore()

    def greet(device):
        pl.semaphore_signal(barrier, inc=1, device_id=(device,), device_id_type=MESH)

    other_blocks(lambda u: greet(member(u, group)))
    other_places(lambda o: greet(16 * block + o))
    other_lines(lambda n: greet(8 * n + spot))
    greet(lax.rem(me + 1, DEVICES))
    greet(lax.rem(me + DEVICES - 1, DEVICES))

    @pl.loop(0, BLOCKS)
    def _(i):
        @pl.when(8 * place + i != me)
        def _():
            greet(8 * place + i)

        @pl.when(16 * i + lax.div(me, 8) != me)
        def _():
            greet(16 * i + lax.div(me, 8))

    stream_copies = [
        pltpu.make_async_copy(streams.at[s], x_own.at[s], local_sem.at[s]) for s in range(SHORT)
    ]
    constant_copies = [
        pltpu.make_async_copy(constants[k], local[k], constant_sem.at[k]) for k in range(CONSTANTS)
    ]
    stream_copies[1].start()
    stream_copies[2].start()
    constant_copies[-1].start()
    constant_copies[-2].start()
    stream_copies[0].start()
    for copy in constant_copies[:-2]:
        copy.start()
    filter_copy = pltpu.make_async_copy(filters, h_own, local_sem.at[3])
    filter_copy.start()

    taps_rows[...] = jnp.zeros_like(taps_rows)
    for s in range(SHORT):
        taps_rows[SHORT * s : SHORT * s + SHORT, :] = taps[s]
    for k in range(D // SIDE):
        cols = taps_rows[:, k * SIDE : (k + 1) * SIDE].T
        taps_cols[k // 4, 4 * (k % 4) : 4 * (k % 4) + 4] = cols.reshape(4, 2, HALF, 16)

    def edge_copy(which):
        return remote(
            edge_out.at[which], edge_in.at[which], edge_sem.at[0, which], edge_sem.at[1, which], lax.rem(me + 1, DEVICES)
        )

    def eight(s, u, h, k):
        return x_own[s, u, 8 * k : 8 * k + 8, h].reshape(SIDE, SIDE)

    def fill_edge(which, width):
        edge = jnp.zeros((SIDE, SIDE), F32)
        for u in range(BLOCKS):
            for h in range(2):
                for k in range(2):
                    if which == 0:
                        got = dot(jnp.concatenate([eight(1, u, h, k), eight(2, u, h, k)], 1), pick[0])
                    else:
                        got = dot(eight(0, u, h, k), pick[1, :SIDE])
                    at = width * (4 * u + 2 * h + k)
                    edge += pltpu.roll(got, at, 1) if at else got
        edge_out[which] = edge.astype(BF16)

    constant_copies[-1].wait()
    constant_copies[-2].wait()
    stream_copies[1].wait()
    stream_copies[2].wait()
    fill_edge(0, 4)

    pl.semaphore_wait(barrier, 2 + BLOCKS - 1 + 2 * (PLACES - 1) + 2 * BLOCKS - 2 * jnp.where(lax.div(me, 8) == place, 1, 0))

    @pl.when(me < DEVICES - 1)
    def _():
        edge_copy(0).start()

    def columns(b):
        return pl.ds(pl.multiple_of(b * BLOCK, BLOCK), BLOCK)

    def input_copy(b, slot):
        return remote(inputs.at[:, columns(b)], i_in.at[slot], group_send.at[2, b], group_recv.at[2, slot], 8 * line + b)

    own_input = pltpu.make_async_copy(inputs.at[:, columns(spot)], i_in.at[spot], local_sem.at[4])
    own_input.start()
    other_spots(lambda b: input_copy(b, spot).start())

    stream_copies[0].wait()
    fill_edge(1, 2)

    @pl.when(me < DEVICES - 1)
    def _():
        edge_copy(1).start()

    filter_copy.wait()
    for m in range(SIDE):
        h_rows[m * OWN : (m + 1) * OWN, :] = h_own[:, m * SIDE : (m + 1) * SIDE]

    def take_edge(which):
        @pl.when(me == 0)
        def _():
            edge_in[which] = jnp.zeros((SIDE, SIDE), BF16)

        @pl.when(me > 0)
        def _():
            edge_copy(which).wait_recv()

        edge_wide[which] = edge_in[which].astype(F32)

    def mixed(s, u, h, k, edge):
        here = eight(s, u, h, k)
        moved = dot(jnp.concatenate([here, edge], 1), shift[s])
        col = taps_cols[u, 8 * k : 8 * k + 8, h].reshape(SIDE, 16)
        total = col[:, 3 * s : 3 * s + 1] * here.astype(F32)
        total = total + col[:, 3 * s + 1 : 3 * s + 2] * moved[:, :SIDE]
        total = total + col[:, 3 * s + 2 : 3 * s + 3] * moved[:, SIDE:]
        return total.astype(BF16)

    def edge_of(which, width, u, h, k):
        at = lax.rem(SIDE - width * (4 * u + 2 * h + k), SIDE)
        return pltpu.roll(edge_wide[which], at, 1).astype(BF16)

    def product_copy(u, slot, h):
        return remote(p_out.at[u, h], p_in.at[slot, h], group_send.at[h, u], group_recv.at[h, slot], member(u, group))

    def query_copy(u, slot):
        return remote(q_out.at[u], q_in.at[slot], group_send.at[3, u], group_recv.at[3, slot], member(u, group))

    def fill_product(ref, u, h):
        for k in range(2):
            edge = edge_of(0, 4, u, h, k)
            value = mixed(1, u, h, k, edge).astype(F32) * mixed(2, u, h, k, edge).astype(F32)
            ref[8 * k : 8 * k + 8] = value.astype(BF16).reshape(8, HALF, SIDE)

    def fill_query(ref, u):
        for h in range(2):
            for k in range(2):
                value = mixed(0, u, h, k, edge_of(1, 2, u, h, k))
                ref[h, 8 * k : 8 * k + 8] = value.reshape(8, HALF, SIDE)

    take_edge(0)

    for h in range(2):
        @other_blocks
        def _(u):
            fill_product(p_out.at[u, h], u, h)
            product_copy(u, block, h).start()

        fill_product(p_in.at[block, h], block, h)

    take_edge(1)

    @other_blocks
    def _(u):
        fill_query(q_out.at[u], u)
        query_copy(u, block).start()

    fill_query(q_in.at[block], block)
    for copy in constant_copies[:-2]:
        copy.wait()

    def pair(ref, c, stride):
        return [ref[pl.ds(c + k, SIDE, stride=stride), :] for k in range(2)]

    def turned(values, sign):
        re, im = values[:SIDE], values[SIDE:]
        cos, sin = turn_re[...], sign * turn_im[...]
        return re * cos - im * sin, re * sin + im * cos

    def swapped(re, im):
        return jnp.concatenate(
            [jnp.concatenate([v[:, k * SIDE : (k + 1) * SIDE] for v in (re, im)], 1) for k in range(2)], 0
        )

    def spectrum_rows(c):
        return pl.ds(pl.multiple_of(c * SIDE, 2 * SIDE), 2 * SIDE)

    def filter_half(h):
        @pl.loop(0, HALF // (2 * PAIRS))
        def _(step):
            starts = [h * HALF + 2 * (PAIRS * step + q) for q in range(PAIRS)]
            values = [jnp.concatenate(pair(h_rows, c, OWN), 1) for c in starts]
            first = [dot(one_h[...], three(v, 0)) for v in values]
            second = [dot(three(swapped(*turned(v, 1.0)), 1), two_x[...]) for v in first]
            for c, v in zip(starts, second):
                h_spec[spectrum_rows(c), :] = v

    def owner_copy(o, slot, h):
        return remote(
            p_in.at[:, h, o], r_in.at[h, slot], block_send.at[h, o], block_recv.at[h, slot], 16 * block + o
        )

    def own_product(h):
        return pltpu.make_async_copy(p_in.at[:, h, place], r_in.at[h, group], local_sem.at[5 + h])

    def forward(h):
        other_blocks(lambda u: product_copy(u, u, h).wait_recv())
        other_places(lambda o: owner_copy(o, group, h).start())
        own_product(h).start()

    def conv_copy(j, slot, h):
        return remote(
            y_out.at[h, j], c_in.at[h, slot], block_send.at[2 + h, j], block_recv.at[2 + h, slot], member(block, j)
        )

    def convolve(h):
        other_groups(lambda j: owner_copy(place, j, h).wait_recv())
        own_product(h).wait()

        @pl.loop(0, PLACES)
        def _(j):
            for u in range(BLOCKS):
                at = pl.multiple_of((j * BLOCKS + u) * HALF, HALF)
                r_rows[pl.ds(at, HALF), :] = r_in[h, j, u].astype(F32)

        @pl.loop(0, HALF // (2 * PAIRS))
        def _(step):
            starts = [2 * (PAIRS * step + q) for q in range(PAIRS)]
            values = [pair(r_rows, c, HALF) for c in starts]
            exact = [jnp.concatenate(v, 1).astype(BF16) for v in values]
            first = [dot(one_x[...], jnp.concatenate([v, v], 0)) for v in exact]
            second = [dot(three(swapped(*turned(v, 1.0)), 1), two_x[...]) for v in first]
            third = []
            for c, v in zip(starts, second):
                other = h_spec[spectrum_rows(h * HALF + c), :]
                x_re, x_im, h_re, h_im = v[:, :SIDE], v[:, SIDE:], other[:, :SIDE], other[:, SIDE:]
                third.append(jnp.concatenate([x_re * h_re - x_im * h_im, x_re * h_im + x_im * h_re], 1))
            third = [dot(three(v, 1), two_y[...]) for v in third]
            third = [
                jnp.concatenate(
                    [
                        jnp.concatenate([v[q * SIDE : (q + 1) * SIDE, p * SIDE : (p + 1) * SIDE] for q in range(2)], 1)
                        for p in range(2)
                    ],
                    0,
                )
                for v in third
            ]
            signal = [dot(one_y[...], three(jnp.concatenate(turned(v, -1.0), 0), 0)) for v in third]
            for c, v, w in zip(starts, values, signal):
                for q in range(2):
                    y_rows[pl.ds(c + q, SIDE, stride=HALF), :] = (
                        w[:, q * SIDE : (q + 1) * SIDE] + gain[h * HALF + c + q] * v[q]
                    )

        def fill_conv(ref, j):
            for u in range(BLOCKS):
                at = pl.multiple_of((j * BLOCKS + u) * HALF, HALF)
                ref[u] = y_rows[pl.ds(at, HALF), :].astype(BF16)

        @other_groups
        def _(j):
            fill_conv(y_out.at[h, j], j)
            conv_copy(j, place, h).start()

        fill_conv(c_in.at[h, place], group)

    def part_rows(o):
        return pl.ds(pl.multiple_of(o * OWN, OWN), OWN)

    def input_part(n, slot):
        return remote(
            part_out.at[0, part_rows(n), :], part_in.at[0, slot], block_send.at[4, n], block_recv.at[4, slot], 8 * n + spot
        )

    def output_part(o, slot):
        return remote(
            part_out.at[1, part_rows(o), :], part_in.at[1, slot], block_send.at[5, o], block_recv.at[5, slot], 16 * block + o
        )

    def input_sum(i, slot):
        return remote(
            fin_out.at[0, i], sums.at[0, slot], fin_send.at[0, i], fin_recv.at[0, slot], 8 * line + i
        )

    def output_sum(i, slot, device):
        return remote(
            fin_out.at[1, i], sums.at[1, slot], fin_send.at[1, i], fin_recv.at[1, slot], device
        )

    def sum_parts(which):
        total = part_in[which, 0].astype(F32)
        for o in range(1, PLACES):
            total += part_in[which, o].astype(F32)
        total = total * (1.0 / (SIDE * SIDE))
        for i in range(BLOCKS):
            fin_out[which, i] = total[4 * i : 4 * i + 4]

    def send_input_parts():
        other_lines(lambda n: input_part(n, line).start())
        part_in[0, line] = part_out[0, part_rows(line), :]

    def send_input_sums():
        other_lines(lambda n: input_part(n, n).wait_recv())
        sum_parts(0)
        other_spots(lambda i: input_sum(i, spot).start())
        sums[0, spot] = fin_out[0, spot]

    def send_output_parts():
        other_places(lambda o: output_part(o, place).start())
        part_in[1, place] = part_out[1, part_rows(place), :]

    def send_output_sums():
        other_places(lambda o: output_part(o, o).wait_recv())
        sum_parts(1)

        @pl.loop(0, BLOCKS)
        def _(i):
            device = 8 * place + i

            @pl.when(device != me)
            def _():
                output_sum(i, block, device).start()

            @pl.when(device == me)
            def _():
                sums[1, block] = fin_out[1, i]

    def wait_sums():
        other_spots(lambda b: input_sum(b, b).wait_recv())

        @pl.loop(0, BLOCKS)
        def _(b):
            @pl.when(16 * b + line != me)
            def _():
                output_sum(0, b, me).wait_recv()

    forward(0)
    filter_half(0)
    forward(1)
    filter_half(1)
    convolve(0)
    convolve(1)

    def gated_copy(u, slot, h):
        return remote(
            g_out.at[u, h], gated.at[slot, :, h], group_send.at[4 + h, u], group_recv.at[4 + h, slot], member(u, group)
        )

    def own_gated(h):
        return pltpu.make_async_copy(g_out.at[block, h], gated.at[block, :, h], local_sem.at[7 + h])

    def fill_gated(u, h):
        value = (q_in[u, h].astype(F32) * c_in[h, :, u].astype(F32)).astype(BF16)
        g_out[u, h] = value
        g_cols[:, h, :, pl.ds(pl.multiple_of(u * SIDE, SIDE), SIDE)] = value

    other_blocks(lambda u: query_copy(u, u).wait_recv())

    def wait_conv(h):
        other_places(lambda o: conv_copy(group, o, h).wait_recv())

    wait_conv(0)

    @other_blocks
    def _(u):
        fill_gated(u, 0)
        gated_copy(u, block, 0).start()

    fill_gated(block, 0)
    own_gated(0).start()
    own_input.wait()
    other_spots(lambda b: input_copy(b, b).wait_recv())
    rows = i_in[...].reshape(BLOCKS * SIDE, BLOCK)
    part_out[0] = dot(rows, rows, ((0,), (0,))).astype(BF16)
    send_input_parts()
    wait_conv(1)
    pl.loop(0, BLOCKS)(lambda u: fill_gated(u, 1))
    columns_all = g_cols[...].reshape(BLOCK, BLOCKS * SIDE)
    part_out[1] = dot(columns_all, columns_all, ((1,), (1,))).astype(BF16)
    send_output_parts()
    other_blocks(lambda u: gated_copy(u, block, 1).start())
    own_gated(1).start()
    send_input_sums()
    send_output_sums()
    wait_sums()

    for h in range(2):
        own_gated(h).wait()

    @other_blocks
    def _(u):
        for h in range(2):
            gated_copy(u, u, h).wait_recv()
            gated_copy(u, u, h).wait_send()
            product_copy(u, u, h).wait_send()
        query_copy(u, u).wait_send()

    @other_spots
    def _(b):
        input_copy(b, b).wait_send()
        input_sum(b, b).wait_send()

    other_lines(lambda n: input_part(n, n).wait_send())

    @other_places
    def _(o):
        for h in range(2):
            owner_copy(o, o, h).wait_send()
        output_part(o, o).wait_send()

    @other_groups
    def _(j):
        for h in range(2):
            conv_copy(j, j, h).wait_send()

    @pl.loop(0, BLOCKS)
    def _(i):
        @pl.when(8 * place + i != me)
        def _():
            output_sum(i, i, me).wait_send()

    @pl.when(me < DEVICES - 1)
    def _():
        for which in range(2):
            edge_copy(which).wait_send()


def write_kernel(got, sums, gated, input_gram, output_gram, held, sems):
    def taken(b):
        return pltpu.make_async_copy(got.at[b], held.at[b], sems.at[0, b])

    def given(b):
        return pltpu.make_async_copy(held.at[b], gated.at[b], sems.at[1, b])

    for b in range(BLOCKS):
        taken(b).start()
    for r in range(BLOCK // DEVICES):
        input_gram[r] = sums[0, :, r, :]
        output_gram[r] = sums[1, :, r, :]
    for b in range(BLOCKS):
        taken(b).wait()
        given(b).start()
    for b in range(BLOCKS):
        given(b).wait()


def body(inputs, streams, short_filter, long_filter, skip_gain):
    anywhere = pl.BlockSpec(memory_space=pl.ANY)
    vmem = pl.BlockSpec(memory_space=pltpu.VMEM)
    smem = pl.BlockSpec(memory_space=pltpu.SMEM)
    constants = tables()
    dma = pltpu.SemaphoreType.DMA
    rows = BLOCK // DEVICES
    split_streams = streams.reshape(SHORT, BLOCKS, PLACES, 2, HALF, SIDE)
    got, sums = pl.pallas_call(
        kernel,
        out_shape=(
            jax.ShapeDtypeStruct((BLOCKS, PLACES, 2, HALF, SIDE), BF16),
            jax.ShapeDtypeStruct((2, BLOCKS, rows, BLOCK), F32),
        ),
        in_specs=[anywhere, anywhere, vmem, anywhere, smem] + [anywhere] * CONSTANTS,
        out_specs=(anywhere, vmem),
        scratch_shapes=[
            pltpu.VMEM((SHORT, BLOCKS, PLACES, 2, HALF, SIDE), BF16),
            pltpu.VMEM((OWN, SIDE * SIDE), F32),
            pltpu.VMEM((16, D), F32),
            pltpu.VMEM((BLOCKS, PLACES, 2, HALF, 16), F32),
            pltpu.VMEM((2, SIDE, SIDE), BF16),
            pltpu.VMEM((2, SIDE, SIDE), BF16),
            pltpu.VMEM((2, SIDE, SIDE), F32),
            pltpu.VMEM((BLOCKS, 2, PLACES, HALF, SIDE), BF16),
            pltpu.VMEM((BLOCKS, 2, PLACES, HALF, SIDE), BF16),
            pltpu.VMEM((BLOCKS, 2, PLACES, HALF, SIDE), BF16),
            pltpu.VMEM((BLOCKS, 2, PLACES, HALF, SIDE), BF16),
            pltpu.VMEM((BLOCKS, SIDE, BLOCK), BF16),
            pltpu.VMEM((2, PLACES, BLOCKS, HALF, SIDE), BF16),
            pltpu.VMEM((SIDE * HALF, SIDE), F32),
            pltpu.VMEM((SIDE * OWN, SIDE), F32),
            pltpu.VMEM((OWN * SIDE, 2 * SIDE), F32),
            pltpu.VMEM((SIDE * HALF, SIDE), F32),
            pltpu.VMEM((2, PLACES, BLOCKS, HALF, SIDE), BF16),
            pltpu.VMEM((2, PLACES, BLOCKS, HALF, SIDE), BF16),
            pltpu.VMEM((BLOCKS, 2, PLACES, HALF, SIDE), BF16),
            pltpu.VMEM((PLACES, 2, HALF, BLOCKS * SIDE), BF16),
            pltpu.VMEM((2, BLOCK, BLOCK), BF16),
            pltpu.VMEM((2, PLACES, OWN, BLOCK), BF16),
            pltpu.VMEM((2, BLOCKS, rows, BLOCK), F32),
            dma((9,)),
            dma((2, 2)),
            dma((6, BLOCKS)),
            dma((6, BLOCKS)),
            dma((6, PLACES)),
            dma((6, PLACES)),
            dma((2, BLOCKS)),
            dma((2, BLOCKS)),
            dma((CONSTANTS,)),
        ]
        + [pltpu.VMEM(c.shape, c.dtype) for c in constants],
        compiler_params=pltpu.CompilerParams(
            collective_id=0, has_side_effects=True, vmem_limit_bytes=56 * 1024 * 1024
        ),
    )(inputs, split_streams, short_filter, long_filter, skip_gain, *[jnp.asarray(c) for c in constants])
    gram = jax.ShapeDtypeStruct((rows, BLOCKS, BLOCK), F32)
    gated, input_gram, output_gram = pl.pallas_call(
        write_kernel,
        out_shape=(jax.ShapeDtypeStruct((BLOCKS, PLACES, 2, HALF, SIDE), BF16), gram, gram),
        in_specs=[anywhere, vmem],
        out_specs=(anywhere, vmem, vmem),
        scratch_shapes=[pltpu.VMEM((BLOCKS, PLACES, 2, HALF, SIDE), BF16), dma((2, BLOCKS))],
    )(got, sums)
    return gated.reshape(D, SIDE), input_gram, output_gram


def solution(mesh):
    in_specs = (P("ctx", None), P(None, None, "ctx"), P(), P("ctx", None), P("ctx"))
    out_specs = (P(None, "ctx"), P("ctx", None, None), P("ctx", None, None))
    return jax.shard_map(body, mesh=mesh, in_specs=in_specs, out_specs=out_specs, check_vma=False)
```

```python
import math

import jax
import jax.numpy as jnp
import numpy as np
from jax import lax
from jax.experimental import pallas as pl
from jax.experimental.pallas import tpu as pltpu
from jax.sharding import PartitionSpec as P

D = 4096
BLOCK = 512
SHORT = 3
DEVICES = 128
BLOCKS = D // BLOCK
PLACES = DEVICES // BLOCKS
OWN = D // DEVICES
HALF = OWN // 2
SIDE = 128
PAIRS = 4
CONSTANTS = 10
F32 = jnp.float32
BF16 = jnp.bfloat16
MESH = pl.DeviceIdType.MESH


def member_of(block, group):
    return 16 * block + 8 * ((group // 8 + block) % 2) + group % 8


def split(values):
    high = np.asarray(values, np.float32).astype(BF16)
    low = (values - high.astype(np.float64)).astype(np.float32).astype(BF16)
    return high, low


def tables():
    index = np.arange(SIDE)
    one = np.exp(2j * math.pi * np.outer(index + 0.25, index) / SIDE)
    turn = np.exp(2j * math.pi * np.outer(index + 0.25, index) / (SIDE * SIDE))
    two = np.exp(2j * math.pi * np.outer(index, index) / SIDE)
    order = np.array([member_of(u, j) for j in range(PLACES) for u in range(BLOCKS)])
    stacked = np.concatenate([one.real, one.imag], 0)
    high, low = split(stacked)
    one_x = np.concatenate([high[:, order], low[:, order]], 1)
    one_h = np.concatenate([high, low, high], 1)
    ahead = np.block([[two.real, two.imag], [-two.imag, two.real]])
    back = np.block([[two.real, -two.imag], [two.imag, two.real]])
    high, low = split(ahead)
    two_x = np.concatenate([high, high, low], 0)
    high, low = split(back)
    two_y = np.concatenate([high, high, low], 0)
    last = stacked.T[order] / (SIDE * SIDE)
    high, low = split(last)
    one_y = np.concatenate([high, low, high], 1)
    turn_re = np.tile(turn.real, (1, 2)).astype(np.float32)
    turn_im = np.tile(turn.imag, (1, 2)).astype(np.float32)
    pick = np.zeros((2, 2 * SIDE, SIDE), np.float32)
    pick[0, SIDE - 2, 0] = pick[0, SIDE - 1, 1] = pick[0, 2 * SIDE - 2, 2] = pick[0, 2 * SIDE - 1, 3] = 1
    pick[1, SIDE - 2, 0] = pick[1, SIDE - 1, 1] = 1
    shift = np.zeros((SHORT, 2 * SIDE, 2 * SIDE), np.float32)
    for s in range(SHORT):
        at = SIDE + (2 if s == 2 else 0)
        shift[s, index[:-1], index[1:]] = 1
        shift[s, index[:-2], SIDE + index[2:]] = 1
        shift[s, at + 1, 0] = shift[s, at, SIDE] = shift[s, at + 1, SIDE + 1] = 1
    rows = np.arange(BLOCK).reshape(BLOCKS, PLACES, BLOCK // DEVICES).swapaxes(0, 1).reshape(-1)
    order = np.eye(BLOCK)[rows].astype(BF16)
    return one_x, one_h, two_x, two_y, one_y, turn_re, turn_im, order, pick.astype(BF16), shift.astype(BF16)


def halves(values):
    high = values.astype(BF16)
    low = (values - high.astype(F32)).astype(BF16)
    return high, low


def three(values, axis):
    high, low = halves(values)
    return jnp.concatenate([high, low, high] if axis else [high, high, low], axis)


def dot(left, right, dims=((1,), (0,))):
    return lax.dot_general(left, right, (dims, ((), ())), preferred_element_type=F32)


def kernel(
    inputs, streams, taps, filters, gain, *rest
):
    constants, rest = rest[:CONSTANTS], rest[CONSTANTS:]
    local, rest = rest[-CONSTANTS:], rest[:-CONSTANTS]
    one_x, one_h, two_x, two_y, one_y, turn_re, turn_im, order, pick, shift = local
    (gated, sums,
    x_own, h_own, taps_rows, taps_cols, edge_out, edge_in, edge_wide,
    p_out, p_in, q_out, q_in, i_in,
    r_in, r_rows, h_rows, h_spec, y_rows, y_out, c_in,
    g_out, g_cols, part_out, part_in, fin_out,
    local_sem, edge_sem, group_send, group_recv, block_send, block_recv, fin_send, fin_recv, constant_sem) = rest
    me = lax.axis_index("ctx")
    block = lax.div(me, 16)
    place = lax.rem(me, 16)
    group = 8 * lax.rem(lax.div(place, 8) + block, 2) + lax.rem(place, 8)
    line, spot = lax.div(me, 8), lax.rem(me, 8)

    def member(b, j):
        return 16 * b + 8 * lax.rem(lax.div(j, 8) + b, 2) + lax.rem(j, 8)

    def remote(src, dst, send, recv, device):
        return pltpu.make_async_remote_copy(
            src_ref=src, dst_ref=dst, send_sem=send, recv_sem=recv, device_id=(device,), device_id_type=MESH
        )

    def other_blocks(step):
        pl.loop(1, BLOCKS)(lambda r: step(lax.rem(block + r, BLOCKS)))

    def other_places(step):
        pl.loop(1, PLACES)(lambda r: step(lax.rem(place + r, PLACES)))

    def other_groups(step):
        pl.loop(1, PLACES)(lambda r: step(lax.rem(group + r, PLACES)))

    def other_lines(step):
        pl.loop(1, PLACES)(lambda r: step(lax.rem(line + r, PLACES)))

    def other_spots(step):
        pl.loop(1, BLOCKS)(lambda r: step(lax.rem(spot + r, BLOCKS)))

    barrier = pltpu.get_barrier_semaphore()

    def greet(device):
        pl.semaphore_signal(barrier, inc=1, device_id=(device,), device_id_type=MESH)

    other_blocks(lambda u: greet(member(u, group)))
    other_places(lambda o: greet(16 * block + o))
    other_lines(lambda n: greet(8 * n + spot))
    greet(lax.rem(me + 1, DEVICES))
    greet(lax.rem(me + DEVICES - 1, DEVICES))

    other_blocks(lambda u: greet(16 * u + place))

    stream_copies = [
        pltpu.make_async_copy(streams.at[s], x_own.at[s], local_sem.at[s]) for s in range(SHORT)
    ]
    constant_copies = [
        pltpu.make_async_copy(constants[k], local[k], constant_sem.at[k]) for k in range(CONSTANTS)
    ]
    stream_copies[1].start()
    stream_copies[2].start()
    constant_copies[-1].start()
    constant_copies[-2].start()
    stream_copies[0].start()
    for copy in constant_copies[:-2]:
        copy.start()
    filter_copy = pltpu.make_async_copy(filters, h_own, local_sem.at[3])
    filter_copy.start()

    taps_rows[...] = jnp.zeros_like(taps_rows)
    for s in range(SHORT):
        taps_rows[SHORT * s : SHORT * s + SHORT, :] = taps[s]
    for k in range(D // SIDE):
        cols = taps_rows[:, k * SIDE : (k + 1) * SIDE].T
        taps_cols[k // 4, 4 * (k % 4) : 4 * (k % 4) + 4] = cols.reshape(4, 2, HALF, 16)

    def edge_copy(which):
        return remote(
            edge_out.at[which], edge_in.at[which], edge_sem.at[0, which], edge_sem.at[1, which], lax.rem(me + 1, DEVICES)
        )

    def eight(s, u, h, k):
        return x_own[s, u, 8 * k : 8 * k + 8, h].reshape(SIDE, SIDE)

    def fill_edge(which, width):
        edge = jnp.zeros((SIDE, SIDE), F32)
        for u in range(BLOCKS):
            for h in range(2):
                for k in range(2):
                    if which == 0:
                        got = dot(jnp.concatenate([eight(1, u, h, k), eight(2, u, h, k)], 1), pick[0])
                    else:
                        got = dot(eight(0, u, h, k), pick[1, :SIDE])
                    at = width * (4 * u + 2 * h + k)
                    edge += pltpu.roll(got, at, 1) if at else got
        edge_out[which] = edge.astype(BF16)

    constant_copies[-1].wait()
    constant_copies[-2].wait()
    stream_copies[1].wait()
    stream_copies[2].wait()
    fill_edge(0, 4)

    pl.semaphore_wait(barrier, 2 + 2 * (BLOCKS - 1) + 2 * (PLACES - 1))

    @pl.when(me < DEVICES - 1)
    def _():
        edge_copy(0).start()

    def columns(b):
        return pl.ds(pl.multiple_of(b * BLOCK, BLOCK), BLOCK)

    def input_copy(b, slot):
        return remote(inputs.at[:, columns(b)], i_in.at[slot], group_send.at[2, b], group_recv.at[2, slot], 8 * line + b)

    own_input = pltpu.make_async_copy(inputs.at[:, columns(spot)], i_in.at[spot], local_sem.at[4])
    own_input.start()
    other_spots(lambda b: input_copy(b, spot).start())

    stream_copies[0].wait()
    fill_edge(1, 2)

    @pl.when(me < DEVICES - 1)
    def _():
        edge_copy(1).start()

    filter_copy.wait()
    for m in range(SIDE):
        h_rows[m * OWN : (m + 1) * OWN, :] = h_own[:, m * SIDE : (m + 1) * SIDE]

    def take_edge(which):
        @pl.when(me == 0)
        def _():
            edge_in[which] = jnp.zeros((SIDE, SIDE), BF16)

        @pl.when(me > 0)
        def _():
            edge_copy(which).wait_recv()

        edge_wide[which] = edge_in[which].astype(F32)

    def mixed(s, u, h, k, edge):
        here = eight(s, u, h, k)
        moved = dot(jnp.concatenate([here, edge], 1), shift[s])
        col = taps_cols[u, 8 * k : 8 * k + 8, h].reshape(SIDE, 16)
        total = col[:, 3 * s : 3 * s + 1] * here.astype(F32)
        total = total + col[:, 3 * s + 1 : 3 * s + 2] * moved[:, :SIDE]
        total = total + col[:, 3 * s + 2 : 3 * s + 3] * moved[:, SIDE:]
        return total.astype(BF16)

    def edge_of(which, width, u, h, k):
        at = lax.rem(SIDE - width * (4 * u + 2 * h + k), SIDE)
        return pltpu.roll(edge_wide[which], at, 1).astype(BF16)

    def product_copy(u, slot, h):
        return remote(p_out.at[u, h], p_in.at[slot, h], group_send.at[h, u], group_recv.at[h, slot], member(u, group))

    def query_copy(u, slot):
        return remote(q_out.at[u], q_in.at[slot], group_send.at[3, u], group_recv.at[3, slot], member(u, group))

    def fill_product(ref, u, h):
        for k in range(2):
            edge = edge_of(0, 4, u, h, k)
            value = mixed(1, u, h, k, edge).astype(F32) * mixed(2, u, h, k, edge).astype(F32)
            ref[8 * k : 8 * k + 8] = value.astype(BF16).reshape(8, HALF, SIDE)

    def fill_query(ref, u):
        for h in range(2):
            for k in range(2):
                value = mixed(0, u, h, k, edge_of(1, 2, u, h, k))
                ref[h, 8 * k : 8 * k + 8] = value.reshape(8, HALF, SIDE)

    take_edge(0)

    for h in range(2):
        @other_blocks
        def _(u):
            fill_product(p_out.at[u, h], u, h)
            product_copy(u, block, h).start()

        fill_product(p_in.at[block, h], block, h)

    take_edge(1)

    @other_blocks
    def _(u):
        fill_query(q_out.at[u], u)
        query_copy(u, block).start()

    fill_query(q_in.at[block], block)
    for copy in constant_copies[:-2]:
        copy.wait()

    def pair(ref, c, stride):
        return [ref[pl.ds(c + k, SIDE, stride=stride), :] for k in range(2)]

    def turned(values, sign):
        re, im = values[:SIDE], values[SIDE:]
        cos, sin = turn_re[...], sign * turn_im[...]
        return re * cos - im * sin, re * sin + im * cos

    def swapped(re, im):
        return jnp.concatenate(
            [jnp.concatenate([v[:, k * SIDE : (k + 1) * SIDE] for v in (re, im)], 1) for k in range(2)], 0
        )

    def spectrum_rows(c):
        return pl.ds(pl.multiple_of(c * SIDE, 2 * SIDE), 2 * SIDE)

    def filter_half(h):
        @pl.loop(0, HALF // (2 * PAIRS))
        def _(step):
            starts = [h * HALF + 2 * (PAIRS * step + q) for q in range(PAIRS)]
            values = [jnp.concatenate(pair(h_rows, c, OWN), 1) for c in starts]
            first = [dot(one_h[...], three(v, 0)) for v in values]
            second = [dot(three(swapped(*turned(v, 1.0)), 1), two_x[...]) for v in first]
            for c, v in zip(starts, second):
                h_spec[spectrum_rows(c), :] = v

    def owner_copy(o, slot, h):
        return remote(
            p_in.at[:, h, o], r_in.at[h, slot], block_send.at[h, o], block_recv.at[h, slot], 16 * block + o
        )

    def own_product(h):
        return pltpu.make_async_copy(p_in.at[:, h, place], r_in.at[h, group], local_sem.at[5 + h])

    def forward(h):
        other_blocks(lambda u: product_copy(u, u, h).wait_recv())
        other_places(lambda o: owner_copy(o, group, h).start())
        own_product(h).start()

    def conv_copy(j, slot, h):
        return remote(
            y_out.at[h, j], c_in.at[h, slot], block_send.at[2 + h, j], block_recv.at[2 + h, slot], member(block, j)
        )

    def convolve(h):
        other_groups(lambda j: owner_copy(place, j, h).wait_recv())
        own_product(h).wait()

        @pl.loop(0, PLACES)
        def _(j):
            for u in range(BLOCKS):
                at = pl.multiple_of((j * BLOCKS + u) * HALF, HALF)
                r_rows[pl.ds(at, HALF), :] = r_in[h, j, u].astype(F32)

        @pl.loop(0, HALF // (2 * PAIRS))
        def _(step):
            starts = [2 * (PAIRS * step + q) for q in range(PAIRS)]
            values = [pair(r_rows, c, HALF) for c in starts]
            exact = [jnp.concatenate(v, 1).astype(BF16) for v in values]
            first = [dot(one_x[...], jnp.concatenate([v, v], 0)) for v in exact]
            second = [dot(three(swapped(*turned(v, 1.0)), 1), two_x[...]) for v in first]
            third = []
            for c, v in zip(starts, second):
                other = h_spec[spectrum_rows(h * HALF + c), :]
                x_re, x_im, h_re, h_im = v[:, :SIDE], v[:, SIDE:], other[:, :SIDE], other[:, SIDE:]
                third.append(jnp.concatenate([x_re * h_re - x_im * h_im, x_re * h_im + x_im * h_re], 1))
            third = [dot(three(v, 1), two_y[...]) for v in third]
            third = [
                jnp.concatenate(
                    [
                        jnp.concatenate([v[q * SIDE : (q + 1) * SIDE, p * SIDE : (p + 1) * SIDE] for q in range(2)], 1)
                        for p in range(2)
                    ],
                    0,
                )
                for v in third
            ]
            signal = [dot(one_y[...], three(jnp.concatenate(turned(v, -1.0), 0), 0)) for v in third]
            for c, v, w in zip(starts, values, signal):
                for q in range(2):
                    y_rows[pl.ds(c + q, SIDE, stride=HALF), :] = (
                        w[:, q * SIDE : (q + 1) * SIDE] + gain[h * HALF + c + q] * v[q]
                    )

        def fill_conv(ref, j):
            for u in range(BLOCKS):
                at = pl.multiple_of((j * BLOCKS + u) * HALF, HALF)
                ref[u] = y_rows[pl.ds(at, HALF), :].astype(BF16)

        @other_groups
        def _(j):
            fill_conv(y_out.at[h, j], j)
            conv_copy(j, place, h).start()

        fill_conv(c_in.at[h, place], group)

    def part_rows(o):
        return pl.ds(pl.multiple_of(o * OWN, OWN), OWN)

    def input_part(n, slot):
        return remote(
            part_out.at[0, part_rows(n), :], part_in.at[0, slot], block_send.at[4, n], block_recv.at[4, slot], 8 * n + spot
        )

    def output_part(o, slot):
        return remote(
            part_out.at[1, part_rows(o), :], part_in.at[1, slot], block_send.at[5, o], block_recv.at[5, slot], 16 * block + o
        )

    def input_sum(i, slot):
        return remote(
            fin_out.at[0, i], sums.at[0, slot], fin_send.at[0, i], fin_recv.at[0, slot], 8 * line + i
        )

    def output_sum(b, slot):
        return remote(
            fin_out.at[1, b], sums.at[1, slot], fin_send.at[1, b], fin_recv.at[1, slot], 16 * b + place
        )

    def sum_parts(which):
        total = part_in[which, 0].astype(F32)
        for o in range(1, PLACES):
            total += part_in[which, o].astype(F32)
        total = total * (1.0 / (SIDE * SIDE))
        for i in range(BLOCKS):
            fin_out[which, i] = total[4 * i : 4 * i + 4]

    def send_input_parts():
        other_lines(lambda n: input_part(n, line).start())
        part_in[0, line] = part_out[0, part_rows(line), :]

    def send_input_sums():
        other_lines(lambda n: input_part(n, n).wait_recv())
        sum_parts(0)
        other_spots(lambda i: input_sum(i, spot).start())
        sums[0, spot] = fin_out[0, spot]

    def send_output_parts():
        other_places(lambda o: output_part(o, place).start())
        part_in[1, place] = part_out[1, part_rows(place), :]

    def send_output_sums():
        other_places(lambda o: output_part(o, o).wait_recv())
        sum_parts(1)
        other_blocks(lambda b: output_sum(b, block).start())
        sums[1, block] = fin_out[1, block]

    def wait_sums():
        other_spots(lambda b: input_sum(b, b).wait_recv())
        other_blocks(lambda b: output_sum(b, b).wait_recv())

    forward(0)
    filter_half(0)
    forward(1)
    filter_half(1)
    convolve(0)
    convolve(1)

    def gated_copy(u, slot, h):
        return remote(
            g_out.at[u, h], gated.at[slot, :, h], group_send.at[4 + h, u], group_recv.at[4 + h, slot], member(u, group)
        )

    def own_gated(h):
        return pltpu.make_async_copy(g_out.at[block, h], gated.at[block, :, h], local_sem.at[7 + h])

    def fill_gated(u, h):
        value = (q_in[u, h].astype(F32) * c_in[h, :, u].astype(F32)).astype(BF16)
        g_out[u, h] = value
        g_cols[:, h, :, pl.ds(pl.multiple_of(u * SIDE, SIDE), SIDE)] = value

    other_blocks(lambda u: query_copy(u, u).wait_recv())

    def wait_conv(h):
        other_places(lambda o: conv_copy(group, o, h).wait_recv())

    wait_conv(0)

    @other_blocks
    def _(u):
        fill_gated(u, 0)
        gated_copy(u, block, 0).start()

    fill_gated(block, 0)
    own_gated(0).start()
    own_input.wait()
    other_spots(lambda b: input_copy(b, b).wait_recv())
    rows = i_in[...].reshape(BLOCKS * SIDE, BLOCK)
    part_out[0] = dot(rows, rows, ((0,), (0,))).astype(BF16)
    send_input_parts()
    wait_conv(1)
    pl.loop(0, BLOCKS)(lambda u: fill_gated(u, 1))
    columns_all = g_cols[...].reshape(BLOCK, BLOCKS * SIDE)
    part = dot(columns_all, columns_all, ((1,), (1,))).astype(BF16)
    part_out[1] = dot(order[...], part).astype(BF16)
    send_output_parts()
    other_blocks(lambda u: gated_copy(u, block, 1).start())
    own_gated(1).start()
    send_input_sums()
    send_output_sums()
    wait_sums()

    for h in range(2):
        own_gated(h).wait()

    @other_blocks
    def _(u):
        for h in range(2):
            gated_copy(u, u, h).wait_recv()
            gated_copy(u, u, h).wait_send()
            product_copy(u, u, h).wait_send()
        query_copy(u, u).wait_send()
        output_sum(u, u).wait_send()

    @other_spots
    def _(b):
        input_copy(b, b).wait_send()
        input_sum(b, b).wait_send()

    other_lines(lambda n: input_part(n, n).wait_send())

    @other_places
    def _(o):
        for h in range(2):
            owner_copy(o, o, h).wait_send()
        output_part(o, o).wait_send()

    @other_groups
    def _(j):
        for h in range(2):
            conv_copy(j, j, h).wait_send()

    @pl.when(me < DEVICES - 1)
    def _():
        for which in range(2):
            edge_copy(which).wait_send()


def write_kernel(got, sums, gated, input_gram, output_gram, held, sems):
    def taken(b):
        return pltpu.make_async_copy(got.at[b], held.at[b], sems.at[0, b])

    def given(b):
        return pltpu.make_async_copy(held.at[b], gated.at[b], sems.at[1, b])

    for b in range(BLOCKS):
        taken(b).start()
    for r in range(BLOCK // DEVICES):
        input_gram[r] = sums[0, :, r, :]
        output_gram[r] = sums[1, :, r, :]
    for b in range(BLOCKS):
        taken(b).wait()
        given(b).start()
    for b in range(BLOCKS):
        given(b).wait()


def body(inputs, streams, short_filter, long_filter, skip_gain):
    anywhere = pl.BlockSpec(memory_space=pl.ANY)
    vmem = pl.BlockSpec(memory_space=pltpu.VMEM)
    smem = pl.BlockSpec(memory_space=pltpu.SMEM)
    constants = tables()
    dma = pltpu.SemaphoreType.DMA
    rows = BLOCK // DEVICES
    split_streams = streams.reshape(SHORT, BLOCKS, PLACES, 2, HALF, SIDE)
    got, sums = pl.pallas_call(
        kernel,
        out_shape=(
            jax.ShapeDtypeStruct((BLOCKS, PLACES, 2, HALF, SIDE), BF16),
            jax.ShapeDtypeStruct((2, BLOCKS, rows, BLOCK), F32),
        ),
        in_specs=[anywhere, anywhere, vmem, anywhere, smem] + [anywhere] * CONSTANTS,
        out_specs=(anywhere, vmem),
        scratch_shapes=[
            pltpu.VMEM((SHORT, BLOCKS, PLACES, 2, HALF, SIDE), BF16),
            pltpu.VMEM((OWN, SIDE * SIDE), F32),
            pltpu.VMEM((16, D), F32),
            pltpu.VMEM((BLOCKS, PLACES, 2, HALF, 16), F32),
            pltpu.VMEM((2, SIDE, SIDE), BF16),
            pltpu.VMEM((2, SIDE, SIDE), BF16),
            pltpu.VMEM((2, SIDE, SIDE), F32),
            pltpu.VMEM((BLOCKS, 2, PLACES, HALF, SIDE), BF16),
            pltpu.VMEM((BLOCKS, 2, PLACES, HALF, SIDE), BF16),
            pltpu.VMEM((BLOCKS, 2, PLACES, HALF, SIDE), BF16),
            pltpu.VMEM((BLOCKS, 2, PLACES, HALF, SIDE), BF16),
            pltpu.VMEM((BLOCKS, SIDE, BLOCK), BF16),
            pltpu.VMEM((2, PLACES, BLOCKS, HALF, SIDE), BF16),
            pltpu.VMEM((SIDE * HALF, SIDE), F32),
            pltpu.VMEM((SIDE * OWN, SIDE), F32),
            pltpu.VMEM((OWN * SIDE, 2 * SIDE), F32),
            pltpu.VMEM((SIDE * HALF, SIDE), F32),
            pltpu.VMEM((2, PLACES, BLOCKS, HALF, SIDE), BF16),
            pltpu.VMEM((2, PLACES, BLOCKS, HALF, SIDE), BF16),
            pltpu.VMEM((BLOCKS, 2, PLACES, HALF, SIDE), BF16),
            pltpu.VMEM((PLACES, 2, HALF, BLOCKS * SIDE), BF16),
            pltpu.VMEM((2, BLOCK, BLOCK), BF16),
            pltpu.VMEM((2, PLACES, OWN, BLOCK), BF16),
            pltpu.VMEM((2, BLOCKS, rows, BLOCK), F32),
            dma((9,)),
            dma((2, 2)),
            dma((6, BLOCKS)),
            dma((6, BLOCKS)),
            dma((6, PLACES)),
            dma((6, PLACES)),
            dma((2, BLOCKS)),
            dma((2, BLOCKS)),
            dma((CONSTANTS,)),
        ]
        + [pltpu.VMEM(c.shape, c.dtype) for c in constants],
        compiler_params=pltpu.CompilerParams(
            collective_id=0, has_side_effects=True, vmem_limit_bytes=56 * 1024 * 1024
        ),
    )(inputs, split_streams, short_filter, long_filter, skip_gain, *[jnp.asarray(c) for c in constants])
    gram = jax.ShapeDtypeStruct((rows, BLOCKS, BLOCK), F32)
    gated, input_gram, output_gram = pl.pallas_call(
        write_kernel,
        out_shape=(jax.ShapeDtypeStruct((BLOCKS, PLACES, 2, HALF, SIDE), BF16), gram, gram),
        in_specs=[anywhere, vmem],
        out_specs=(anywhere, vmem, vmem),
        scratch_shapes=[pltpu.VMEM((BLOCKS, PLACES, 2, HALF, SIDE), BF16), dma((2, BLOCKS))],
    )(got, sums)
    return gated.reshape(D, SIDE), input_gram, output_gram


def solution(mesh):
    in_specs = (P("ctx", None), P(None, None, "ctx"), P(), P("ctx", None), P("ctx"))
    out_specs = (P(None, "ctx"), P("ctx", None, None), P("ctx", None, None))
    return jax.shard_map(body, mesh=mesh, in_specs=in_specs, out_specs=out_specs, check_vma=False)
```

```python
import math

import jax
import jax.numpy as jnp
import numpy as np
from jax import lax
from jax.experimental import pallas as pl
from jax.experimental.pallas import tpu as pltpu
from jax.sharding import PartitionSpec as P

D = 4096
BLOCK = 512
SHORT = 3
DEVICES = 128
BLOCKS = D // BLOCK
PLACES = DEVICES // BLOCKS
OWN = D // DEVICES
HALF = OWN // 2
SIDE = 128
PAIRS = 4
CONSTANTS = 10
F32 = jnp.float32
BF16 = jnp.bfloat16
MESH = pl.DeviceIdType.MESH


def member_of(block, group):
    return 16 * block + 8 * ((group // 8 + block) % 2) + group % 8


def split(values):
    high = np.asarray(values, np.float32).astype(BF16)
    low = (values - high.astype(np.float64)).astype(np.float32).astype(BF16)
    return high, low


def tables():
    index = np.arange(SIDE)
    one = np.exp(2j * math.pi * np.outer(index + 0.25, index) / SIDE)
    turn = np.exp(2j * math.pi * np.outer(index + 0.25, index) / (SIDE * SIDE))
    two = np.exp(2j * math.pi * np.outer(index, index) / SIDE)
    order = np.array([member_of(u, j) for j in range(PLACES) for u in range(BLOCKS)])
    stacked = np.concatenate([one.real, one.imag], 0)
    high, low = split(stacked)
    one_x = np.concatenate([high[:, order], low[:, order]], 1)
    one_h = np.concatenate([high, low, high], 1)
    ahead = np.block([[two.real, two.imag], [-two.imag, two.real]])
    back = np.block([[two.real, -two.imag], [two.imag, two.real]])
    high, low = split(ahead)
    two_x = np.concatenate([high, high, low], 0)
    high, low = split(back)
    two_y = np.concatenate([high, high, low], 0)
    last = stacked.T[order] / (SIDE * SIDE)
    high, low = split(last)
    one_y = np.concatenate([high, low, high], 1)
    turn_re = np.tile(turn.real, (1, 2)).astype(np.float32)
    turn_im = np.tile(turn.imag, (1, 2)).astype(np.float32)
    pick = np.zeros((2, 2 * SIDE, SIDE), np.float32)
    pick[0, SIDE - 2, 0] = pick[0, SIDE - 1, 1] = pick[0, 2 * SIDE - 2, 2] = pick[0, 2 * SIDE - 1, 3] = 1
    pick[1, SIDE - 2, 0] = pick[1, SIDE - 1, 1] = 1
    shift = np.zeros((SHORT, 2 * SIDE, 2 * SIDE), np.float32)
    for s in range(SHORT):
        at = SIDE + (2 if s == 2 else 0)
        shift[s, index[:-1], index[1:]] = 1
        shift[s, index[:-2], SIDE + index[2:]] = 1
        shift[s, at + 1, 0] = shift[s, at, SIDE] = shift[s, at + 1, SIDE + 1] = 1
    rows = np.arange(BLOCK).reshape(BLOCKS, PLACES, BLOCK // DEVICES).swapaxes(0, 1).reshape(-1)
    order = np.eye(BLOCK)[rows].astype(BF16)
    return one_x, one_h, two_x, two_y, one_y, turn_re, turn_im, order, pick.astype(BF16), shift.astype(BF16)


def halves(values):
    high = values.astype(BF16)
    low = (values - high.astype(F32)).astype(BF16)
    return high, low


def three(values, axis):
    high, low = halves(values)
    return jnp.concatenate([high, low, high] if axis else [high, high, low], axis)


def dot(left, right, dims=((1,), (0,))):
    return lax.dot_general(left, right, (dims, ((), ())), preferred_element_type=F32)


def kernel(
    inputs, streams, taps, filters, gain, *rest
):
    constants, rest = rest[:CONSTANTS], rest[CONSTANTS:]
    local, rest = rest[-CONSTANTS:], rest[:-CONSTANTS]
    one_x, one_h, two_x, two_y, one_y, turn_re, turn_im, order, pick, shift = local
    (gated, sums,
    x_own, h_own, taps_rows, taps_cols, edge_out, edge_in, edge_wide,
    p_out, p_in, q_out, q_in, i_in,
    r_in, r_rows, h_rows, h_spec, y_rows, y_out, c_in,
    g_out, g_cols, part_out, part_in, fin_out,
    local_sem, edge_sem, group_send, group_recv, block_send, block_recv, fin_send, fin_recv, constant_sem) = rest
    me = lax.axis_index("ctx")
    block = lax.div(me, 16)
    place = lax.rem(me, 16)
    group = 8 * lax.rem(lax.div(place, 8) + block, 2) + lax.rem(place, 8)
    line, spot = lax.div(me, 8), lax.rem(me, 8)

    def member(b, j):
        return 16 * b + 8 * lax.rem(lax.div(j, 8) + b, 2) + lax.rem(j, 8)

    def remote(src, dst, send, recv, device):
        return pltpu.make_async_remote_copy(
            src_ref=src, dst_ref=dst, send_sem=send, recv_sem=recv, device_id=(device,), device_id_type=MESH
        )

    def other_blocks(step):
        pl.loop(1, BLOCKS)(lambda r: step(lax.rem(block + r, BLOCKS)))

    def other_places(step):
        pl.loop(1, PLACES)(lambda r: step(lax.rem(place + r, PLACES)))

    def other_groups(step):
        pl.loop(1, PLACES)(lambda r: step(lax.rem(group + r, PLACES)))

    def other_lines(step):
        pl.loop(1, PLACES)(lambda r: step(lax.rem(line + r, PLACES)))

    def other_spots(step):
        pl.loop(1, BLOCKS)(lambda r: step(lax.rem(spot + r, BLOCKS)))

    barrier = pltpu.get_barrier_semaphore()

    def greet(device):
        pl.semaphore_signal(barrier, inc=1, device_id=(device,), device_id_type=MESH)

    other_blocks(lambda u: greet(member(u, group)))
    other_places(lambda o: greet(16 * block + o))
    other_lines(lambda n: greet(8 * n + spot))
    greet(lax.rem(me + 1, DEVICES))
    greet(lax.rem(me + DEVICES - 1, DEVICES))

    other_blocks(lambda u: greet(16 * u + place))

    stream_copies = [
        pltpu.make_async_copy(streams.at[s], x_own.at[s], local_sem.at[s]) for s in range(SHORT)
    ]
    constant_copies = [
        pltpu.make_async_copy(constants[k], local[k], constant_sem.at[k]) for k in range(CONSTANTS)
    ]
    stream_copies[1].start()
    stream_copies[2].start()
    constant_copies[-1].start()
    constant_copies[-2].start()
    stream_copies[0].start()
    for copy in constant_copies[:-2]:
        copy.start()
    filter_copy = pltpu.make_async_copy(filters, h_own, local_sem.at[3])
    filter_copy.start()

    taps_rows[...] = jnp.zeros_like(taps_rows)
    for s in range(SHORT):
        taps_rows[SHORT * s : SHORT * s + SHORT, :] = taps[s]
    for k in range(D // SIDE):
        cols = taps_rows[:, k * SIDE : (k + 1) * SIDE].T
        taps_cols[k // 4, 4 * (k % 4) : 4 * (k % 4) + 4] = cols.reshape(4, 2, HALF, 16)

    def edge_copy(which):
        return remote(
            edge_out.at[which], edge_in.at[which], edge_sem.at[0, which], edge_sem.at[1, which], lax.rem(me + 1, DEVICES)
        )

    def eight(s, u, h, k):
        return x_own[s, u, 8 * k : 8 * k + 8, h].reshape(SIDE, SIDE)

    def fill_edge(which, width):
        edge = jnp.zeros((SIDE, SIDE), F32)
        for u in range(BLOCKS):
            for h in range(2):
                for k in range(2):
                    if which == 0:
                        got = dot(jnp.concatenate([eight(1, u, h, k), eight(2, u, h, k)], 1), pick[0])
                    else:
                        got = dot(eight(0, u, h, k), pick[1, :SIDE])
                    at = width * (4 * u + 2 * h + k)
                    edge += pltpu.roll(got, at, 1) if at else got
        edge_out[which] = edge.astype(BF16)

    constant_copies[-1].wait()
    constant_copies[-2].wait()
    stream_copies[1].wait()
    stream_copies[2].wait()
    fill_edge(0, 4)
    stream_copies[0].wait()
    fill_edge(1, 2)

    pl.semaphore_wait(barrier, 2 + 2 * (BLOCKS - 1) + 2 * (PLACES - 1))

    @pl.when(me < DEVICES - 1)
    def _():
        edge_copy(0).start()
        edge_copy(1).start()

    def columns(b):
        return pl.ds(pl.multiple_of(b * BLOCK, BLOCK), BLOCK)

    def input_copy(b, slot):
        return remote(inputs.at[:, columns(b)], i_in.at[slot], group_send.at[2, b], group_recv.at[2, slot], 8 * line + b)

    own_input = pltpu.make_async_copy(inputs.at[:, columns(spot)], i_in.at[spot], local_sem.at[4])
    own_input.start()
    other_spots(lambda b: input_copy(b, spot).start())


    filter_copy.wait()
    for m in range(SIDE):
        h_rows[m * OWN : (m + 1) * OWN, :] = h_own[:, m * SIDE : (m + 1) * SIDE]

    def take_edge(which):
        @pl.when(me == 0)
        def _():
            edge_in[which] = jnp.zeros((SIDE, SIDE), BF16)

        @pl.when(me > 0)
        def _():
            edge_copy(which).wait_recv()

        edge_wide[which] = edge_in[which].astype(F32)

    def mixed(s, u, h, k, edge):
        here = eight(s, u, h, k)
        moved = dot(jnp.concatenate([here, edge], 1), shift[s])
        col = taps_cols[u, 8 * k : 8 * k + 8, h].reshape(SIDE, 16)
        total = col[:, 3 * s : 3 * s + 1] * here.astype(F32)
        total = total + col[:, 3 * s + 1 : 3 * s + 2] * moved[:, :SIDE]
        total = total + col[:, 3 * s + 2 : 3 * s + 3] * moved[:, SIDE:]
        return total.astype(BF16)

    def edge_of(which, width, u, h, k):
        at = lax.rem(SIDE - width * (4 * u + 2 * h + k), SIDE)
        return pltpu.roll(edge_wide[which], at, 1).astype(BF16)

    def product_copy(u, slot, h):
        return remote(p_out.at[u, h], p_in.at[slot, h], group_send.at[h, u], group_recv.at[h, slot], member(u, group))

    def query_copy(u, slot):
        return remote(q_out.at[u], q_in.at[slot], group_send.at[3, u], group_recv.at[3, slot], member(u, group))

    def fill_product(ref, u, h):
        for k in range(2):
            edge = edge_of(0, 4, u, h, k)
            value = mixed(1, u, h, k, edge).astype(F32) * mixed(2, u, h, k, edge).astype(F32)
            ref[8 * k : 8 * k + 8] = value.astype(BF16).reshape(8, HALF, SIDE)

    def fill_query(ref, u):
        for h in range(2):
            for k in range(2):
                value = mixed(0, u, h, k, edge_of(1, 2, u, h, k))
                ref[h, 8 * k : 8 * k + 8] = value.reshape(8, HALF, SIDE)

    take_edge(0)

    for h in range(2):
        @other_blocks
        def _(u):
            fill_product(p_out.at[u, h], u, h)
            product_copy(u, block, h).start()

        fill_product(p_in.at[block, h], block, h)

    take_edge(1)

    @other_blocks
    def _(u):
        fill_query(q_out.at[u], u)

    fill_query(q_in.at[block], block)
    for copy in constant_copies[:-2]:
        copy.wait()

    def pair(ref, c, stride):
        return [ref[pl.ds(c + k, SIDE, stride=stride), :] for k in range(2)]

    def turned(values, sign):
        re, im = values[:SIDE], values[SIDE:]
        cos, sin = turn_re[...], sign * turn_im[...]
        return re * cos - im * sin, re * sin + im * cos

    def swapped(re, im):
        return jnp.concatenate(
            [jnp.concatenate([v[:, k * SIDE : (k + 1) * SIDE] for v in (re, im)], 1) for k in range(2)], 0
        )

    def spectrum_rows(c):
        return pl.ds(pl.multiple_of(c * SIDE, 2 * SIDE), 2 * SIDE)

    def filter_half(h):
        @pl.loop(0, HALF // (2 * PAIRS))
        def _(step):
            starts = [h * HALF + 2 * (PAIRS * step + q) for q in range(PAIRS)]
            values = [jnp.concatenate(pair(h_rows, c, OWN), 1) for c in starts]
            first = [dot(one_h[...], three(v, 0)) for v in values]
            second = [dot(three(swapped(*turned(v, 1.0)), 1), two_x[...]) for v in first]
            for c, v in zip(starts, second):
                h_spec[spectrum_rows(c), :] = v

    def owner_copy(o, slot, h):
        return remote(
            p_in.at[:, h, o], r_in.at[h, slot], block_send.at[h, o], block_recv.at[h, slot], 16 * block + o
        )

    def own_product(h):
        return pltpu.make_async_copy(p_in.at[:, h, place], r_in.at[h, group], local_sem.at[5 + h])

    def forward(h):
        other_blocks(lambda u: product_copy(u, u, h).wait_recv())
        other_places(lambda o: owner_copy(o, group, h).start())
        own_product(h).start()

    def conv_copy(j, slot, h):
        return remote(
            y_out.at[h, j], c_in.at[h, slot], block_send.at[2 + h, j], block_recv.at[2 + h, slot], member(block, j)
        )

    def convolve(h):
        other_groups(lambda j: owner_copy(place, j, h).wait_recv())
        own_product(h).wait()

        @pl.loop(0, PLACES)
        def _(j):
            for u in range(BLOCKS):
                at = pl.multiple_of((j * BLOCKS + u) * HALF, HALF)
                r_rows[pl.ds(at, HALF), :] = r_in[h, j, u].astype(F32)

        @pl.loop(0, HALF // (2 * PAIRS))
        def _(step):
            starts = [2 * (PAIRS * step + q) for q in range(PAIRS)]
            values = [pair(r_rows, c, HALF) for c in starts]
            exact = [jnp.concatenate(v, 1).astype(BF16) for v in values]
            first = [dot(one_x[...], jnp.concatenate([v, v], 0)) for v in exact]
            second = [dot(three(swapped(*turned(v, 1.0)), 1), two_x[...]) for v in first]
            third = []
            for c, v in zip(starts, second):
                other = h_spec[spectrum_rows(h * HALF + c), :]
                x_re, x_im, h_re, h_im = v[:, :SIDE], v[:, SIDE:], other[:, :SIDE], other[:, SIDE:]
                third.append(jnp.concatenate([x_re * h_re - x_im * h_im, x_re * h_im + x_im * h_re], 1))
            third = [dot(three(v, 1), two_y[...]) for v in third]
            third = [
                jnp.concatenate(
                    [
                        jnp.concatenate([v[q * SIDE : (q + 1) * SIDE, p * SIDE : (p + 1) * SIDE] for q in range(2)], 1)
                        for p in range(2)
                    ],
                    0,
                )
                for v in third
            ]
            signal = [dot(one_y[...], three(jnp.concatenate(turned(v, -1.0), 0), 0)) for v in third]
            for c, v, w in zip(starts, values, signal):
                for q in range(2):
                    y_rows[pl.ds(c + q, SIDE, stride=HALF), :] = (
                        w[:, q * SIDE : (q + 1) * SIDE] + gain[h * HALF + c + q] * v[q]
                    )

        def fill_conv(ref, j):
            for u in range(BLOCKS):
                at = pl.multiple_of((j * BLOCKS + u) * HALF, HALF)
                ref[u] = y_rows[pl.ds(at, HALF), :].astype(BF16)

        @other_groups
        def _(j):
            fill_conv(y_out.at[h, j], j)
            conv_copy(j, place, h).start()

        fill_conv(c_in.at[h, place], group)

    def part_rows(o):
        return pl.ds(pl.multiple_of(o * OWN, OWN), OWN)

    def input_part(n, slot):
        return remote(
            part_out.at[0, part_rows(n), :], part_in.at[0, slot], block_send.at[4, n], block_recv.at[4, slot], 8 * n + spot
        )

    def output_part(o, slot):
        return remote(
            part_out.at[1, part_rows(o), :], part_in.at[1, slot], block_send.at[5, o], block_recv.at[5, slot], 16 * block + o
        )

    def input_sum(i, slot):
        return remote(
            fin_out.at[0, i], sums.at[0, slot], fin_send.at[0, i], fin_recv.at[0, slot], 8 * line + i
        )

    def output_sum(b, slot):
        return remote(
            fin_out.at[1, b], sums.at[1, slot], fin_send.at[1, b], fin_recv.at[1, slot], 16 * b + place
        )

    def sum_parts(which):
        total = part_in[which, 0].astype(F32)
        for o in range(1, PLACES):
            total += part_in[which, o].astype(F32)
        total = total * (1.0 / (SIDE * SIDE))
        for i in range(BLOCKS):
            fin_out[which, i] = total[4 * i : 4 * i + 4]

    def send_input_parts():
        other_lines(lambda n: input_part(n, line).start())
        part_in[0, line] = part_out[0, part_rows(line), :]

    def send_input_sums():
        other_lines(lambda n: input_part(n, n).wait_recv())
        sum_parts(0)
        other_spots(lambda i: input_sum(i, spot).start())
        sums[0, spot] = fin_out[0, spot]

    def send_output_parts():
        other_places(lambda o: output_part(o, place).start())
        part_in[1, place] = part_out[1, part_rows(place), :]

    def send_output_sums():
        other_places(lambda o: output_part(o, o).wait_recv())
        sum_parts(1)
        other_blocks(lambda b: output_sum(b, block).start())
        sums[1, block] = fin_out[1, block]

    def wait_sums():
        other_spots(lambda b: input_sum(b, b).wait_recv())
        other_blocks(lambda b: output_sum(b, b).wait_recv())

    forward(0)
    filter_half(0)
    forward(1)
    other_blocks(lambda u: query_copy(u, block).start())
    filter_half(1)
    convolve(0)
    convolve(1)

    def gated_copy(u, slot, h):
        return remote(
            g_out.at[u, h], gated.at[slot, :, h], group_send.at[4 + h, u], group_recv.at[4 + h, slot], member(u, group)
        )

    def own_gated(h):
        return pltpu.make_async_copy(g_out.at[block, h], gated.at[block, :, h], local_sem.at[7 + h])

    def fill_gated(u, h):
        value = (q_in[u, h].astype(F32) * c_in[h, :, u].astype(F32)).astype(BF16)
        g_out[u, h] = value
        g_cols[:, h, :, pl.ds(pl.multiple_of(u * SIDE, SIDE), SIDE)] = value

    other_blocks(lambda u: query_copy(u, u).wait_recv())

    def wait_conv(h):
        other_places(lambda o: conv_copy(group, o, h).wait_recv())

    wait_conv(0)

    @other_blocks
    def _(u):
        fill_gated(u, 0)
        gated_copy(u, block, 0).start()

    fill_gated(block, 0)
    own_gated(0).start()
    own_input.wait()
    other_spots(lambda b: input_copy(b, b).wait_recv())
    rows = i_in[...].reshape(BLOCKS * SIDE, BLOCK)
    part_out[0] = dot(rows, rows, ((0,), (0,))).astype(BF16)
    send_input_parts()
    wait_conv(1)
    pl.loop(0, BLOCKS)(lambda u: fill_gated(u, 1))
    columns_all = g_cols[...].reshape(BLOCK, BLOCKS * SIDE)
    part = dot(columns_all, columns_all, ((1,), (1,))).astype(BF16)
    part_out[1] = dot(order[...], part).astype(BF16)
    send_output_parts()
    other_blocks(lambda u: gated_copy(u, block, 1).start())
    own_gated(1).start()
    send_input_sums()
    send_output_sums()
    wait_sums()

    for h in range(2):
        own_gated(h).wait()

    @other_blocks
    def _(u):
        for h in range(2):
            gated_copy(u, u, h).wait_recv()
            gated_copy(u, u, h).wait_send()
            product_copy(u, u, h).wait_send()
        query_copy(u, u).wait_send()
        output_sum(u, u).wait_send()

    @other_spots
    def _(b):
        input_copy(b, b).wait_send()
        input_sum(b, b).wait_send()

    other_lines(lambda n: input_part(n, n).wait_send())

    @other_places
    def _(o):
        for h in range(2):
            owner_copy(o, o, h).wait_send()
        output_part(o, o).wait_send()

    @other_groups
    def _(j):
        for h in range(2):
            conv_copy(j, j, h).wait_send()

    @pl.when(me < DEVICES - 1)
    def _():
        for which in range(2):
            edge_copy(which).wait_send()


def write_kernel(got, sums, gated, input_gram, output_gram, held, sems):
    def taken(b):
        return pltpu.make_async_copy(got.at[b], held.at[b], sems.at[0, b])

    def given(b):
        return pltpu.make_async_copy(held.at[b], gated.at[b], sems.at[1, b])

    for b in range(BLOCKS):
        taken(b).start()
    for r in range(BLOCK // DEVICES):
        input_gram[r] = sums[0, :, r, :]
        output_gram[r] = sums[1, :, r, :]
    for b in range(BLOCKS):
        taken(b).wait()
        given(b).start()
    for b in range(BLOCKS):
        given(b).wait()


def body(inputs, streams, short_filter, long_filter, skip_gain):
    anywhere = pl.BlockSpec(memory_space=pl.ANY)
    vmem = pl.BlockSpec(memory_space=pltpu.VMEM)
    smem = pl.BlockSpec(memory_space=pltpu.SMEM)
    constants = tables()
    dma = pltpu.SemaphoreType.DMA
    rows = BLOCK // DEVICES
    split_streams = streams.reshape(SHORT, BLOCKS, PLACES, 2, HALF, SIDE)
    got, sums = pl.pallas_call(
        kernel,
        out_shape=(
            jax.ShapeDtypeStruct((BLOCKS, PLACES, 2, HALF, SIDE), BF16),
            jax.ShapeDtypeStruct((2, BLOCKS, rows, BLOCK), F32),
        ),
        in_specs=[anywhere, anywhere, vmem, anywhere, smem] + [anywhere] * CONSTANTS,
        out_specs=(anywhere, vmem),
        scratch_shapes=[
            pltpu.VMEM((SHORT, BLOCKS, PLACES, 2, HALF, SIDE), BF16),
            pltpu.VMEM((OWN, SIDE * SIDE), F32),
            pltpu.VMEM((16, D), F32),
            pltpu.VMEM((BLOCKS, PLACES, 2, HALF, 16), F32),
            pltpu.VMEM((2, SIDE, SIDE), BF16),
            pltpu.VMEM((2, SIDE, SIDE), BF16),
            pltpu.VMEM((2, SIDE, SIDE), F32),
            pltpu.VMEM((BLOCKS, 2, PLACES, HALF, SIDE), BF16),
            pltpu.VMEM((BLOCKS, 2, PLACES, HALF, SIDE), BF16),
            pltpu.VMEM((BLOCKS, 2, PLACES, HALF, SIDE), BF16),
            pltpu.VMEM((BLOCKS, 2, PLACES, HALF, SIDE), BF16),
            pltpu.VMEM((BLOCKS, SIDE, BLOCK), BF16),
            pltpu.VMEM((2, PLACES, BLOCKS, HALF, SIDE), BF16),
            pltpu.VMEM((SIDE * HALF, SIDE), F32),
            pltpu.VMEM((SIDE * OWN, SIDE), F32),
            pltpu.VMEM((OWN * SIDE, 2 * SIDE), F32),
            pltpu.VMEM((SIDE * HALF, SIDE), F32),
            pltpu.VMEM((2, PLACES, BLOCKS, HALF, SIDE), BF16),
            pltpu.VMEM((2, PLACES, BLOCKS, HALF, SIDE), BF16),
            pltpu.VMEM((BLOCKS, 2, PLACES, HALF, SIDE), BF16),
            pltpu.VMEM((PLACES, 2, HALF, BLOCKS * SIDE), BF16),
            pltpu.VMEM((2, BLOCK, BLOCK), BF16),
            pltpu.VMEM((2, PLACES, OWN, BLOCK), BF16),
            pltpu.VMEM((2, BLOCKS, rows, BLOCK), F32),
            dma((9,)),
            dma((2, 2)),
            dma((6, BLOCKS)),
            dma((6, BLOCKS)),
            dma((6, PLACES)),
            dma((6, PLACES)),
            dma((2, BLOCKS)),
            dma((2, BLOCKS)),
            dma((CONSTANTS,)),
        ]
        + [pltpu.VMEM(c.shape, c.dtype) for c in constants],
        compiler_params=pltpu.CompilerParams(
            collective_id=0, has_side_effects=True, vmem_limit_bytes=56 * 1024 * 1024
        ),
    )(inputs, split_streams, short_filter, long_filter, skip_gain, *[jnp.asarray(c) for c in constants])
    gram = jax.ShapeDtypeStruct((rows, BLOCKS, BLOCK), F32)
    gated, input_gram, output_gram = pl.pallas_call(
        write_kernel,
        out_shape=(jax.ShapeDtypeStruct((BLOCKS, PLACES, 2, HALF, SIDE), BF16), gram, gram),
        in_specs=[anywhere, vmem],
        out_specs=(anywhere, vmem, vmem),
        scratch_shapes=[pltpu.VMEM((BLOCKS, PLACES, 2, HALF, SIDE), BF16), dma((2, BLOCKS))],
    )(got, sums)
    return gated.reshape(D, SIDE), input_gram, output_gram


def solution(mesh):
    in_specs = (P("ctx", None), P(None, None, "ctx"), P(), P("ctx", None), P("ctx"))
    out_specs = (P(None, "ctx"), P("ctx", None, None), P("ctx", None, None))
    return jax.shard_map(body, mesh=mesh, in_specs=in_specs, out_specs=out_specs, check_vma=False)
```

```python
import math

import jax
import jax.numpy as jnp
import numpy as np
from jax import lax
from jax.experimental import pallas as pl
from jax.experimental.pallas import tpu as pltpu
from jax.sharding import PartitionSpec as P

D = 4096
BLOCK = 512
SHORT = 3
DEVICES = 128
BLOCKS = D // BLOCK
PLACES = DEVICES // BLOCKS
OWN = D // DEVICES
HALF = OWN // 2
SIDE = 128
PAIRS = 8
CONSTANTS = 10
F32 = jnp.float32
BF16 = jnp.bfloat16
MESH = pl.DeviceIdType.MESH


def member_of(block, group):
    return 16 * block + 8 * ((group // 8 + block) % 2) + group % 8


def split(values):
    high = np.asarray(values, np.float32).astype(BF16)
    low = (values - high.astype(np.float64)).astype(np.float32).astype(BF16)
    return high, low


def tables():
    index = np.arange(SIDE)
    one = np.exp(2j * math.pi * np.outer(index + 0.25, index) / SIDE)
    turn = np.exp(2j * math.pi * np.outer(index + 0.25, index) / (SIDE * SIDE))
    two = np.exp(2j * math.pi * np.outer(index, index) / SIDE)
    order = np.array([member_of(u, j) for j in range(PLACES) for u in range(BLOCKS)])
    stacked = np.concatenate([one.real, one.imag], 0)
    high, low = split(stacked)
    one_x = np.concatenate([high[:, order], low[:, order]], 1)
    one_h = np.concatenate([high, low, high], 1)
    ahead = np.block([[two.real, two.imag], [-two.imag, two.real]])
    back = np.block([[two.real, -two.imag], [two.imag, two.real]])
    high, low = split(ahead)
    two_x = np.concatenate([high, high, low], 0)
    high, low = split(back)
    two_y = np.concatenate([high, high, low], 0)
    last = stacked.T[order] / (SIDE * SIDE)
    high, low = split(last)
    one_y = np.concatenate([high, low, high], 1)
    turn_re = np.tile(turn.real, (1, 2)).astype(np.float32)
    turn_im = np.tile(turn.imag, (1, 2)).astype(np.float32)
    pick = np.zeros((2, 2 * SIDE, SIDE), np.float32)
    pick[0, SIDE - 2, 0] = pick[0, SIDE - 1, 1] = pick[0, 2 * SIDE - 2, 2] = pick[0, 2 * SIDE - 1, 3] = 1
    pick[1, SIDE - 2, 0] = pick[1, SIDE - 1, 1] = 1
    shift = np.zeros((SHORT, 2 * SIDE, 2 * SIDE), np.float32)
    for s in range(SHORT):
        at = SIDE + (2 if s == 2 else 0)
        shift[s, index[:-1], index[1:]] = 1
        shift[s, index[:-2], SIDE + index[2:]] = 1
        shift[s, at + 1, 0] = shift[s, at, SIDE] = shift[s, at + 1, SIDE + 1] = 1
    rows = np.arange(BLOCK).reshape(BLOCKS, PLACES, BLOCK // DEVICES).swapaxes(0, 1).reshape(-1)
    order = np.eye(BLOCK)[rows].astype(BF16)
    return one_x, one_h, two_x, two_y, one_y, turn_re, turn_im, order, pick.astype(BF16), shift.astype(BF16)


def halves(values):
    high = values.astype(BF16)
    low = (values - high.astype(F32)).astype(BF16)
    return high, low


def three(values, axis):
    high, low = halves(values)
    return jnp.concatenate([high, low, high] if axis else [high, high, low], axis)


def dot(left, right, dims=((1,), (0,))):
    return lax.dot_general(left, right, (dims, ((), ())), preferred_element_type=F32)


def kernel(
    inputs, streams, taps, filters, gain, *rest
):
    constants, rest = rest[:CONSTANTS], rest[CONSTANTS:]
    local, rest = rest[-CONSTANTS:], rest[:-CONSTANTS]
    one_x, one_h, two_x, two_y, one_y, turn_re, turn_im, order, pick, shift = local
    (gated, sums,
    x_own, h_own, taps_rows, taps_cols, edge_out, edge_in, edge_wide,
    p_out, p_in, q_out, q_in, i_in,
    r_in, r_rows, h_rows, h_spec, y_rows, y_out, c_in,
    g_out, g_cols, part_out, part_in, fin_out,
    local_sem, edge_sem, group_send, group_recv, block_send, block_recv, fin_send, fin_recv, constant_sem) = rest
    me = lax.axis_index("ctx")
    block = lax.div(me, 16)
    place = lax.rem(me, 16)
    group = 8 * lax.rem(lax.div(place, 8) + block, 2) + lax.rem(place, 8)
    line, spot = lax.div(me, 8), lax.rem(me, 8)

    def member(b, j):
        return 16 * b + 8 * lax.rem(lax.div(j, 8) + b, 2) + lax.rem(j, 8)

    def remote(src, dst, send, recv, device):
        return pltpu.make_async_remote_copy(
            src_ref=src, dst_ref=dst, send_sem=send, recv_sem=recv, device_id=(device,), device_id_type=MESH
        )

    def other_blocks(step):
        pl.loop(1, BLOCKS, unroll=True)(lambda r: step(lax.rem(block + r, BLOCKS)))

    def other_places(step):
        pl.loop(1, PLACES, unroll=True)(lambda r: step(lax.rem(place + r, PLACES)))

    def other_groups(step):
        pl.loop(1, PLACES, unroll=True)(lambda r: step(lax.rem(group + r, PLACES)))

    def other_lines(step):
        pl.loop(1, PLACES, unroll=True)(lambda r: step(lax.rem(line + r, PLACES)))

    def other_spots(step):
        pl.loop(1, BLOCKS, unroll=True)(lambda r: step(lax.rem(spot + r, BLOCKS)))

    barrier = pltpu.get_barrier_semaphore()

    def greet(device):
        pl.semaphore_signal(barrier, inc=1, device_id=(device,), device_id_type=MESH)

    other_blocks(lambda u: greet(member(u, group)))
    other_places(lambda o: greet(16 * block + o))
    other_lines(lambda n: greet(8 * n + spot))
    greet(lax.rem(me + 1, DEVICES))
    greet(lax.rem(me + DEVICES - 1, DEVICES))

    other_blocks(lambda u: greet(16 * u + place))

    stream_copies = [
        pltpu.make_async_copy(streams.at[s], x_own.at[s], local_sem.at[s]) for s in range(SHORT)
    ]
    constant_copies = [
        pltpu.make_async_copy(constants[k], local[k], constant_sem.at[k]) for k in range(CONSTANTS)
    ]
    stream_copies[1].start()
    stream_copies[2].start()
    constant_copies[-1].start()
    constant_copies[-2].start()
    stream_copies[0].start()
    for copy in constant_copies[:-2]:
        copy.start()
    filter_copy = pltpu.make_async_copy(filters, h_own, local_sem.at[3])
    filter_copy.start()

    taps_rows[...] = jnp.zeros_like(taps_rows)
    for s in range(SHORT):
        taps_rows[SHORT * s : SHORT * s + SHORT, :] = taps[s]
    for k in range(D // SIDE):
        cols = taps_rows[:, k * SIDE : (k + 1) * SIDE].T
        taps_cols[k // 4, 4 * (k % 4) : 4 * (k % 4) + 4] = cols.reshape(4, 2, HALF, 16)

    def edge_copy(which):
        return remote(
            edge_out.at[which], edge_in.at[which], edge_sem.at[0, which], edge_sem.at[1, which], lax.rem(me + 1, DEVICES)
        )

    def eight(s, u, h, k):
        return x_own[s, u, 8 * k : 8 * k + 8, h].reshape(SIDE, SIDE)

    def fill_edge(which, width):
        edge = jnp.zeros((SIDE, SIDE), F32)
        for u in range(BLOCKS):
            for h in range(2):
                for k in range(2):
                    if which == 0:
                        got = dot(jnp.concatenate([eight(1, u, h, k), eight(2, u, h, k)], 1), pick[0])
                    else:
                        got = dot(eight(0, u, h, k), pick[1, :SIDE])
                    at = width * (4 * u + 2 * h + k)
                    edge += pltpu.roll(got, at, 1) if at else got
        edge_out[which] = edge.astype(BF16)

    constant_copies[-1].wait()
    constant_copies[-2].wait()
    stream_copies[1].wait()
    stream_copies[2].wait()
    fill_edge(0, 4)
    stream_copies[0].wait()
    fill_edge(1, 2)

    pl.semaphore_wait(barrier, 2 + 2 * (BLOCKS - 1) + 2 * (PLACES - 1))

    @pl.when(me < DEVICES - 1)
    def _():
        edge_copy(0).start()
        edge_copy(1).start()

    def columns(b):
        return pl.ds(pl.multiple_of(b * BLOCK, BLOCK), BLOCK)

    def input_copy(b, slot):
        return remote(inputs.at[:, columns(b)], i_in.at[slot], group_send.at[2, b], group_recv.at[2, slot], 8 * line + b)

    own_input = pltpu.make_async_copy(inputs.at[:, columns(spot)], i_in.at[spot], local_sem.at[4])
    own_input.start()
    other_spots(lambda b: input_copy(b, spot).start())


    filter_copy.wait()
    for m in range(SIDE):
        h_rows[m * OWN : (m + 1) * OWN, :] = h_own[:, m * SIDE : (m + 1) * SIDE]

    def take_edge(which):
        @pl.when(me == 0)
        def _():
            edge_in[which] = jnp.zeros((SIDE, SIDE), BF16)

        @pl.when(me > 0)
        def _():
            edge_copy(which).wait_recv()

        edge_wide[which] = edge_in[which].astype(F32)

    def mixed(s, u, h, k, edge):
        here = eight(s, u, h, k)
        moved = dot(jnp.concatenate([here, edge], 1), shift[s])
        col = taps_cols[u, 8 * k : 8 * k + 8, h].reshape(SIDE, 16)
        total = col[:, 3 * s : 3 * s + 1] * here.astype(F32)
        total = total + col[:, 3 * s + 1 : 3 * s + 2] * moved[:, :SIDE]
        total = total + col[:, 3 * s + 2 : 3 * s + 3] * moved[:, SIDE:]
        return total.astype(BF16)

    def edge_of(which, width, u, h, k):
        at = lax.rem(SIDE - width * (4 * u + 2 * h + k), SIDE)
        return pltpu.roll(edge_wide[which], at, 1).astype(BF16)

    def product_copy(u, slot, h):
        return remote(p_out.at[u, h], p_in.at[slot, h], group_send.at[h, u], group_recv.at[h, slot], member(u, group))

    def query_copy(u, slot):
        return remote(q_out.at[u], q_in.at[slot], group_send.at[3, u], group_recv.at[3, slot], member(u, group))

    def fill_product(ref, u, h):
        for k in range(2):
            edge = edge_of(0, 4, u, h, k)
            value = mixed(1, u, h, k, edge).astype(F32) * mixed(2, u, h, k, edge).astype(F32)
            ref[8 * k : 8 * k + 8] = value.astype(BF16).reshape(8, HALF, SIDE)

    def fill_query(ref, u):
        for h in range(2):
            for k in range(2):
                value = mixed(0, u, h, k, edge_of(1, 2, u, h, k))
                ref[h, 8 * k : 8 * k + 8] = value.reshape(8, HALF, SIDE)

    take_edge(0)

    for h in range(2):
        @other_blocks
        def _(u):
            fill_product(p_out.at[u, h], u, h)
            product_copy(u, block, h).start()

        fill_product(p_in.at[block, h], block, h)

    take_edge(1)

    @other_blocks
    def _(u):
        fill_query(q_out.at[u], u)

    fill_query(q_in.at[block], block)
    for copy in constant_copies[:-2]:
        copy.wait()

    def pair(ref, c, stride):
        return [ref[pl.ds(c + k, SIDE, stride=stride), :] for k in range(2)]

    def turned(values, sign):
        re, im = values[:SIDE], values[SIDE:]
        cos, sin = turn_re[...], sign * turn_im[...]
        return re * cos - im * sin, re * sin + im * cos

    def swapped(re, im):
        return jnp.concatenate(
            [jnp.concatenate([v[:, k * SIDE : (k + 1) * SIDE] for v in (re, im)], 1) for k in range(2)], 0
        )

    def spectrum_rows(c):
        return pl.ds(pl.multiple_of(c * SIDE, 2 * SIDE), 2 * SIDE)

    def filter_half(h):
        @pl.loop(0, HALF // (2 * PAIRS))
        def _(step):
            starts = [h * HALF + 2 * (PAIRS * step + q) for q in range(PAIRS)]
            values = [jnp.concatenate(pair(h_rows, c, OWN), 1) for c in starts]
            first = [dot(one_h[...], three(v, 0)) for v in values]
            second = [dot(three(swapped(*turned(v, 1.0)), 1), two_x[...]) for v in first]
            for c, v in zip(starts, second):
                h_spec[spectrum_rows(c), :] = v

    def owner_copy(o, slot, h):
        return remote(
            p_in.at[:, h, o], r_in.at[h, slot], block_send.at[h, o], block_recv.at[h, slot], 16 * block + o
        )

    def own_product(h):
        return pltpu.make_async_copy(p_in.at[:, h, place], r_in.at[h, group], local_sem.at[5 + h])

    def forward(h):
        other_blocks(lambda u: product_copy(u, u, h).wait_recv())
        other_places(lambda o: owner_copy(o, group, h).start())
        own_product(h).start()

    def conv_copy(j, slot, h):
        return remote(
            y_out.at[h, j], c_in.at[h, slot], block_send.at[2 + h, j], block_recv.at[2 + h, slot], member(block, j)
        )

    def convolve(h):
        other_groups(lambda j: owner_copy(place, j, h).wait_recv())
        own_product(h).wait()

        @pl.loop(0, PLACES)
        def _(j):
            for u in range(BLOCKS):
                at = pl.multiple_of((j * BLOCKS + u) * HALF, HALF)
                r_rows[pl.ds(at, HALF), :] = r_in[h, j, u].astype(F32)

        @pl.loop(0, HALF // (2 * PAIRS))
        def _(step):
            starts = [2 * (PAIRS * step + q) for q in range(PAIRS)]
            values = [pair(r_rows, c, HALF) for c in starts]
            exact = [jnp.concatenate(v, 1).astype(BF16) for v in values]
            first = [dot(one_x[...], jnp.concatenate([v, v], 0)) for v in exact]
            second = [dot(three(swapped(*turned(v, 1.0)), 1), two_x[...]) for v in first]
            third = []
            for c, v in zip(starts, second):
                other = h_spec[spectrum_rows(h * HALF + c), :]
                x_re, x_im, h_re, h_im = v[:, :SIDE], v[:, SIDE:], other[:, :SIDE], other[:, SIDE:]
                third.append(jnp.concatenate([x_re * h_re - x_im * h_im, x_re * h_im + x_im * h_re], 1))
            third = [dot(three(v, 1), two_y[...]) for v in third]
            third = [
                jnp.concatenate(
                    [
                        jnp.concatenate([v[q * SIDE : (q + 1) * SIDE, p * SIDE : (p + 1) * SIDE] for q in range(2)], 1)
                        for p in range(2)
                    ],
                    0,
                )
                for v in third
            ]
            signal = [dot(one_y[...], three(jnp.concatenate(turned(v, -1.0), 0), 0)) for v in third]
            for c, v, w in zip(starts, values, signal):
                for q in range(2):
                    y_rows[pl.ds(c + q, SIDE, stride=HALF), :] = (
                        w[:, q * SIDE : (q + 1) * SIDE] + gain[h * HALF + c + q] * v[q]
                    )

        def fill_conv(ref, j):
            for u in range(BLOCKS):
                at = pl.multiple_of((j * BLOCKS + u) * HALF, HALF)
                ref[u] = y_rows[pl.ds(at, HALF), :].astype(BF16)

        @other_groups
        def _(j):
            fill_conv(y_out.at[h, j], j)
            conv_copy(j, place, h).start()

        fill_conv(c_in.at[h, place], group)

    def part_rows(o):
        return pl.ds(pl.multiple_of(o * OWN, OWN), OWN)

    def input_part(n, slot):
        return remote(
            part_out.at[0, part_rows(n), :], part_in.at[0, slot], block_send.at[4, n], block_recv.at[4, slot], 8 * n + spot
        )

    def output_part(o, slot):
        return remote(
            part_out.at[1, part_rows(o), :], part_in.at[1, slot], block_send.at[5, o], block_recv.at[5, slot], 16 * block + o
        )

    def input_sum(i, slot):
        return remote(
            fin_out.at[0, i], sums.at[0, slot], fin_send.at[0, i], fin_recv.at[0, slot], 8 * line + i
        )

    def output_sum(b, slot):
        return remote(
            fin_out.at[1, b], sums.at[1, slot], fin_send.at[1, b], fin_recv.at[1, slot], 16 * b + place
        )

    def sum_parts(which):
        total = part_in[which, 0].astype(F32)
        for o in range(1, PLACES):
            total += part_in[which, o].astype(F32)
        total = total * (1.0 / (SIDE * SIDE))
        for i in range(BLOCKS):
            fin_out[which, i] = total[4 * i : 4 * i + 4]

    def send_input_parts():
        other_lines(lambda n: input_part(n, line).start())
        part_in[0, line] = part_out[0, part_rows(line), :]

    def send_input_sums():
        other_lines(lambda n: input_part(n, n).wait_recv())
        sum_parts(0)
        other_spots(lambda i: input_sum(i, spot).start())
        sums[0, spot] = fin_out[0, spot]

    def send_output_parts():
        other_places(lambda o: output_part(o, place).start())
        part_in[1, place] = part_out[1, part_rows(place), :]

    def send_output_sums():
        other_places(lambda o: output_part(o, o).wait_recv())
        sum_parts(1)
        other_blocks(lambda b: output_sum(b, block).start())
        sums[1, block] = fin_out[1, block]

    def wait_sums():
        other_spots(lambda b: input_sum(b, b).wait_recv())
        other_blocks(lambda b: output_sum(b, b).wait_recv())

    forward(0)
    filter_half(0)
    forward(1)
    other_blocks(lambda u: query_copy(u, block).start())
    filter_half(1)
    convolve(0)
    convolve(1)

    def gated_copy(u, slot, h):
        return remote(
            g_out.at[u, h], gated.at[slot, :, h], group_send.at[4 + h, u], group_recv.at[4 + h, slot], member(u, group)
        )

    def own_gated(h):
        return pltpu.make_async_copy(g_out.at[block, h], gated.at[block, :, h], local_sem.at[7 + h])

    def fill_gated(u, h):
        value = (q_in[u, h].astype(F32) * c_in[h, :, u].astype(F32)).astype(BF16)
        g_out[u, h] = value
        g_cols[:, h, :, pl.ds(pl.multiple_of(u * SIDE, SIDE), SIDE)] = value

    other_blocks(lambda u: query_copy(u, u).wait_recv())

    def wait_conv(h):
        other_places(lambda o: conv_copy(group, o, h).wait_recv())

    wait_conv(0)

    @other_blocks
    def _(u):
        fill_gated(u, 0)
        gated_copy(u, block, 0).start()

    fill_gated(block, 0)
    own_gated(0).start()
    own_input.wait()
    other_spots(lambda b: input_copy(b, b).wait_recv())
    rows = i_in[...].reshape(BLOCKS * SIDE, BLOCK)
    part_out[0] = dot(rows, rows, ((0,), (0,))).astype(BF16)
    send_input_parts()
    @other_blocks
    def _(u):
        for h in range(2):
            product_copy(u, u, h).wait_send()
        query_copy(u, u).wait_send()

    @other_places
    def _(o):
        for h in range(2):
            owner_copy(o, o, h).wait_send()

    other_spots(lambda b: input_copy(b, b).wait_send())

    @pl.when(me < DEVICES - 1)
    def _():
        for which in range(2):
            edge_copy(which).wait_send()

    wait_conv(1)
    pl.loop(0, BLOCKS)(lambda u: fill_gated(u, 1))
    columns_all = g_cols[...].reshape(BLOCK, BLOCKS * SIDE)
    part = dot(columns_all, columns_all, ((1,), (1,))).astype(BF16)
    part_out[1] = dot(order[...], part).astype(BF16)
    send_output_parts()
    other_blocks(lambda u: gated_copy(u, block, 1).start())
    own_gated(1).start()
    send_input_sums()
    send_output_sums()
    wait_sums()

    for h in range(2):
        own_gated(h).wait()

    @other_blocks
    def _(u):
        for h in range(2):
            gated_copy(u, u, h).wait_recv()
            gated_copy(u, u, h).wait_send()
        output_sum(u, u).wait_send()

    other_spots(lambda b: input_sum(b, b).wait_send())
    other_lines(lambda n: input_part(n, n).wait_send())
    other_places(lambda o: output_part(o, o).wait_send())

    @other_groups
    def _(j):
        for h in range(2):
            conv_copy(j, j, h).wait_send()


def write_kernel(got, sums, gated, input_gram, output_gram, held, sems):
    def taken(b):
        return pltpu.make_async_copy(got.at[b], held.at[b], sems.at[0, b])

    def given(b):
        return pltpu.make_async_copy(held.at[b], gated.at[b], sems.at[1, b])

    for b in range(BLOCKS):
        taken(b).start()
    for r in range(BLOCK // DEVICES):
        input_gram[r] = sums[0, :, r, :]
        output_gram[r] = sums[1, :, r, :]
    for b in range(BLOCKS):
        taken(b).wait()
        given(b).start()
    for b in range(BLOCKS):
        given(b).wait()


def body(inputs, streams, short_filter, long_filter, skip_gain):
    anywhere = pl.BlockSpec(memory_space=pl.ANY)
    vmem = pl.BlockSpec(memory_space=pltpu.VMEM)
    smem = pl.BlockSpec(memory_space=pltpu.SMEM)
    constants = tables()
    dma = pltpu.SemaphoreType.DMA
    rows = BLOCK // DEVICES
    split_streams = streams.reshape(SHORT, BLOCKS, PLACES, 2, HALF, SIDE)
    got, sums = pl.pallas_call(
        kernel,
        out_shape=(
            jax.ShapeDtypeStruct((BLOCKS, PLACES, 2, HALF, SIDE), BF16),
            jax.ShapeDtypeStruct((2, BLOCKS, rows, BLOCK), F32),
        ),
        in_specs=[anywhere, anywhere, vmem, anywhere, smem] + [anywhere] * CONSTANTS,
        out_specs=(anywhere, vmem),
        scratch_shapes=[
            pltpu.VMEM((SHORT, BLOCKS, PLACES, 2, HALF, SIDE), BF16),
            pltpu.VMEM((OWN, SIDE * SIDE), F32),
            pltpu.VMEM((16, D), F32),
            pltpu.VMEM((BLOCKS, PLACES, 2, HALF, 16), F32),
            pltpu.VMEM((2, SIDE, SIDE), BF16),
            pltpu.VMEM((2, SIDE, SIDE), BF16),
            pltpu.VMEM((2, SIDE, SIDE), F32),
            pltpu.VMEM((BLOCKS, 2, PLACES, HALF, SIDE), BF16),
            pltpu.VMEM((BLOCKS, 2, PLACES, HALF, SIDE), BF16),
            pltpu.VMEM((BLOCKS, 2, PLACES, HALF, SIDE), BF16),
            pltpu.VMEM((BLOCKS, 2, PLACES, HALF, SIDE), BF16),
            pltpu.VMEM((BLOCKS, SIDE, BLOCK), BF16),
            pltpu.VMEM((2, PLACES, BLOCKS, HALF, SIDE), BF16),
            pltpu.VMEM((SIDE * HALF, SIDE), F32),
            pltpu.VMEM((SIDE * OWN, SIDE), F32),
            pltpu.VMEM((OWN * SIDE, 2 * SIDE), F32),
            pltpu.VMEM((SIDE * HALF, SIDE), F32),
            pltpu.VMEM((2, PLACES, BLOCKS, HALF, SIDE), BF16),
            pltpu.VMEM((2, PLACES, BLOCKS, HALF, SIDE), BF16),
            pltpu.VMEM((BLOCKS, 2, PLACES, HALF, SIDE), BF16),
            pltpu.VMEM((PLACES, 2, HALF, BLOCKS * SIDE), BF16),
            pltpu.VMEM((2, BLOCK, BLOCK), BF16),
            pltpu.VMEM((2, PLACES, OWN, BLOCK), BF16),
            pltpu.VMEM((2, BLOCKS, rows, BLOCK), F32),
            dma((9,)),
            dma((2, 2)),
            dma((6, BLOCKS)),
            dma((6, BLOCKS)),
            dma((6, PLACES)),
            dma((6, PLACES)),
            dma((2, BLOCKS)),
            dma((2, BLOCKS)),
            dma((CONSTANTS,)),
        ]
        + [pltpu.VMEM(c.shape, c.dtype) for c in constants],
        compiler_params=pltpu.CompilerParams(
            collective_id=0, has_side_effects=True, vmem_limit_bytes=56 * 1024 * 1024
        ),
    )(inputs, split_streams, short_filter, long_filter, skip_gain, *[jnp.asarray(c) for c in constants])
    gram = jax.ShapeDtypeStruct((rows, BLOCKS, BLOCK), F32)
    gated, input_gram, output_gram = pl.pallas_call(
        write_kernel,
        out_shape=(jax.ShapeDtypeStruct((BLOCKS, PLACES, 2, HALF, SIDE), BF16), gram, gram),
        in_specs=[anywhere, vmem],
        out_specs=(anywhere, vmem, vmem),
        scratch_shapes=[pltpu.VMEM((BLOCKS, PLACES, 2, HALF, SIDE), BF16), dma((2, BLOCKS))],
    )(got, sums)
    return gated.reshape(D, SIDE), input_gram, output_gram


def solution(mesh):
    in_specs = (P("ctx", None), P(None, None, "ctx"), P(), P("ctx", None), P("ctx"))
    out_specs = (P(None, "ctx"), P("ctx", None, None), P("ctx", None, None))
    return jax.shard_map(body, mesh=mesh, in_specs=in_specs, out_specs=out_specs, check_vma=False)
```
